32 devices in a mesh: groups: 2 (over x), refl: 8 (over z, y), freq: 2 (over core).
Axes of the slice: x: 2, y: 2, z: 4, core: 2. Of those that a mesh axis runs over, the one named last changes fastest.
Arguments:
- spectra: bfloat16 [2, 16, 1024, 8192], P(None, 'freq', 'groups', 'refl'), parts along dimension 2, may hold values from -9 to 9
- recorded: bfloat16 [8, 2, 64, 64, 256], P('refl', 'freq', 'groups'), parts along dimension 2, may hold values from -10 to 10
- initial_filters: float32 [8, 2, 2, 2, 33], P('refl', 'freq', 'groups'), parts along dimension 2, may hold values from -0.6 to 0.6
Outputs:
- primaries: bfloat16 [8, 2, 64, 64, 256], P('refl', 'freq', 'groups'), parts along dimension 2
- filters: float32 [8, 2, 2, 2, 33], P('refl', 'freq', 'groups'), parts along dimension 2
The draws below stay inside these ranges and needn't reach their ends.
There are 2 independent parts, one for each index of `groups`. The reference program is written for one: setup_inputs(seed, part) draws one part's arguments, and reference() takes and returns one part's arrays. A program takes and returns all parts, laid end to end along the dimension named above; each array names one. Nothing has to cross between parts.
All inputs are finite; a program needn't handle non-finite values.
Results may differ from the reference program's by a relative error of at most 0.025.
Values may be sent and summed in bfloat16 or wider, within the bound.
No kernel may reach another device: no remote copies, remote signals or barrier semaphores. Data moves between devices by JAX's collectives and lax.ppermute only.
A program may use at most 128 MiB of HBM per device.

```python
import math
import jax
import jax.numpy as jnp
from jax import lax

NF = 16
K0 = 48
NT = 256
XR = 8192
TS = 32
TR = 64
WC = 32
WM = 4
TAPS = 33
ITERS = 3
FB = 2
ST = 2
NS = 64
NR = 512
N_REFL = 8
N_FREQ = 2


def make_spectra(key):
    noise_key, scale_key = jax.random.split(jax.random.fold_in(key, 17))
    noise = jax.random.truncated_normal(noise_key, -3.0, 3.0, (2, NF, NR, XR), jnp.float32)
    spread = jnp.exp(jax.random.uniform(scale_key, (1, 1, NR, 1), jnp.float32, 0.0, math.log(8.0))) / 2.8
    return (noise * spread).astype(jnp.bfloat16)


def draw_spectra(key, part):
    return make_spectra(key)


def predicted_traces(key):
    spectra = make_spectra(key).astype(jnp.float32)
    real_full = spectra[0]
    imaginary_full = spectra[1]
    block_width = math.gcd(XR, 256)
    block_count = XR // block_width
    amplitude = 1.0 / math.sqrt(2.0 * XR)
    highest_precision = lax.Precision.HIGHEST

    def add_block(block_index, running):
        real_totals, imaginary_totals = running
        first_point = (block_index * block_width).astype(jnp.int32)
        real_block_piece = lax.dynamic_slice_in_dim(real_full, first_point, block_width, 2)
        imaginary_block_piece = lax.dynamic_slice_in_dim(imaginary_full, first_point, block_width, 2)
        real_source_rows = real_block_piece[:, :NS]
        imaginary_source_rows = imaginary_block_piece[:, :NS]
        real_portion = jnp.einsum('hvt,hkt->hvk', real_source_rows, real_block_piece, precision=highest_precision) - jnp.einsum('hvt,hkt->hvk', imaginary_source_rows, imaginary_block_piece, precision=highest_precision)
        imaginary_portion = jnp.einsum('hvt,hkt->hvk', real_source_rows, imaginary_block_piece, precision=highest_precision) + jnp.einsum('hvt,hkt->hvk', imaginary_source_rows, real_block_piece, precision=highest_precision)
        return (real_totals + real_portion, imaginary_totals + imaginary_portion)
    zeros_start = jnp.zeros((NF, NS, NR), jnp.float32)
    real_totals, imaginary_totals = lax.fori_loop(0, block_count, add_block, (zeros_start, zeros_start))
    frequency_bins = jnp.arange(NF, dtype=jnp.int32)
    samples = jnp.arange(NT, dtype=jnp.int32)
    phases = (K0 + frequency_bins)[:, None] * samples[None, :] % NT
    angles = 2.0 * math.pi / NT * phases.astype(jnp.float32)
    weight = amplitude * math.sqrt(2.0 / NF)
    cosine_table = weight * jnp.cos(angles)
    sine_table = -weight * jnp.sin(angles)
    return jnp.einsum('mwb,mx->wbx', real_totals, cosine_table, precision=highest_precision) + jnp.einsum('mwb,mx->wbx', imaginary_totals, sine_table, precision=highest_precision)


def draw_recorded(key, part):
    multiples = predicted_traces(key)
    noise_key, scale_key = jax.random.split(jax.random.fold_in(key, 29))
    taps_key, gain_key = jax.random.split(jax.random.fold_in(key, 31))
    half_taps = (TAPS - 1) // 2
    true_taps = 0.08 * jax.random.normal(taps_key, (NS // WC, NR // WC, TAPS), jnp.float32)
    window_gain = jnp.exp(jax.random.uniform(gain_key, (NS // WC, NR // WC, 1), jnp.float32, math.log(0.5), math.log(2.0)))
    true_taps = true_taps * window_gain
    convolved = jnp.zeros((NS, NR, NT), jnp.float32)
    for tap_number in range(TAPS):
        shifted = jnp.roll(multiples, tap_number - half_taps, axis=2)
        tap_grid = jnp.repeat(jnp.repeat(true_taps[:, :, tap_number], WC, axis=0), WC, axis=1)
        convolved = convolved + tap_grid[:, :, None] * shifted
    noise = jax.random.truncated_normal(noise_key, -3.0, 3.0, (NS, NR, NT), jnp.float32)
    spread = jnp.exp(jax.random.uniform(scale_key, (NS, NR, 1), jnp.float32, 0.0, math.log(10.0))) / 4.0
    total = jnp.clip(convolved + noise * spread, -10.0, 10.0)
    tiles = total.reshape(ST, TS, 4 * FB, TR, NT)
    tiles = jnp.transpose(tiles, (0, 2, 1, 3, 4)).reshape(4 * ST * FB, TS, TR, NT)
    tiles = jnp.roll(tiles, -2 * FB, axis=0).reshape(4 * ST, FB, TS, TR, NT)
    return tiles.astype(jnp.bfloat16)


def block_levels(key, extent, cuts, low, high):
    factor_of = 1.0
    for dim, parts in cuts:
        draws = jax.random.uniform(jax.random.fold_in(jax.random.fold_in(key, 6), dim), (parts,), jnp.float32, low / len(cuts), high / len(cuts))
        factor_of = factor_of * jnp.repeat(jnp.exp(draws), extent[dim] // parts).reshape((-1,) + (1,) * (len(extent) - 1 - dim))
    return factor_of


def centred(stream_key, extent, deviation, bound, pieces=(), held_as=jnp.bfloat16):
    array = deviation * jax.random.normal(stream_key, extent, jnp.float32)
    if pieces:
        array = array * block_levels(stream_key, extent, pieces, -0.22, 0.18)
    return jnp.clip(array, -bound, bound).astype(held_as)


def setup_inputs(seed: int = 0, part: int = 0) -> dict:
    arg_keys = jax.random.split(jax.random.key(seed), 4)
    part_keys = jax.random.split(jax.random.fold_in(arg_keys[3], part), 4)
    return {
        "spectra": draw_spectra(jax.random.fold_in(jax.random.fold_in(arg_keys[3], part), 71), part),
        "recorded": draw_recorded(jax.random.fold_in(jax.random.fold_in(arg_keys[3], part), 71), part),
        "initial_filters": centred(part_keys[2], (N_REFL, N_FREQ, TS // WC, TR // WC, TAPS), 0.15, 0.6, ((0, 8), (1, 2)), jnp.float32),
    }


EXACT_PRECISION = lax.Precision.HIGHEST

def time_table():
    frequency_bins = jnp.arange(NF, dtype=jnp.int32)
    samples = jnp.arange(NT, dtype=jnp.int32)
    phases = (K0 + frequency_bins)[:, None] * samples[None, :] % NT
    angles = 2.0 * math.pi / NT * phases.astype(jnp.float32)
    weight = math.sqrt(2.0 / NF)
    return jnp.stack([weight * jnp.cos(angles), -weight * jnp.sin(angles)], axis=1).astype(jnp.bfloat16)

def lag_sums(matrix):
    length = matrix.shape[-1]
    leading = matrix.shape[:-2]
    doubled = jnp.concatenate([matrix, matrix], axis=-1).reshape(leading + (2 * length * length,))
    padded = jnp.concatenate([doubled, jnp.zeros(leading + (length,), matrix.dtype)], axis=-1)
    skewed = padded.reshape(leading + (length, 2 * length + 1))
    return lax.optimization_barrier(jnp.sum(skewed, axis=-2))[..., :length]

def solve_filters(gram_sums, cross_sums, initial):
    length = gram_sums.shape[-1]
    half_taps = (TAPS - 1) // 2
    lag_gram = lag_sums(gram_sums)[..., :TAPS]
    lag_cross = lag_sums(cross_sums)
    target = jnp.concatenate([jnp.flip(lag_cross[..., :half_taps + 1], -1), jnp.flip(lag_cross[..., length - half_taps:], -1)], -1)
    row_bound = lag_gram[..., 0] + 2.0 * lax.optimization_barrier(jnp.sum(jnp.abs(lag_gram[..., 1:]), -1))
    step_size = 0.5 / (row_bound + 1e-06)
    tap_index = jnp.arange(TAPS, dtype=jnp.int32)
    offset = jnp.abs(tap_index[:, None] - tap_index[None, :])
    select = (offset[:, :, None] == tap_index[None, None, :]).astype(jnp.float32)
    toeplitz = jnp.einsum('abk,...k->...ab', select, lag_gram, precision=EXACT_PRECISION)
    filters = initial
    for repeat in range(ITERS):
        applied = jnp.einsum('...ab,...b->...a', toeplitz, filters, precision=EXACT_PRECISION)
        filters = filters + step_size[..., None] * (target - applied)
    return filters

def conv_matrix(taps):
    half_taps = (TAPS - 1) // 2
    positions = jnp.arange(NT, dtype=jnp.int32)
    circular_shift = (positions[None, :] - positions[:, None]) % NT
    wanted = (jnp.arange(TAPS, dtype=jnp.int32) - half_taps) % NT
    select = (circular_shift[None] == wanted[:, None, None]).astype(jnp.float32)
    return jnp.einsum('kut,...k->...ut', select, taps.astype(jnp.float32), precision=EXACT_PRECISION).astype(jnp.bfloat16)

def to_grid(tiles):
    source_rows = N_REFL // 4
    columns = 4 * N_FREQ
    shape = tiles.shape
    flat = tiles.reshape((N_REFL * N_FREQ,) + shape[2:])
    flat = jnp.roll(flat, 2 * N_FREQ, axis=0)
    grouped = flat.reshape((source_rows, columns) + shape[2:])
    order = (0, 2, 1, 3) + tuple(range(4, grouped.ndim))
    moved = jnp.transpose(grouped, order)
    return moved.reshape((source_rows * shape[2], columns * shape[3]) + shape[4:])

def from_grid(grid, across, along):
    source_rows = N_REFL // 4
    columns = 4 * N_FREQ
    rest = grid.shape[2:]
    split = grid.reshape((source_rows, across, columns, along) + rest)
    order = (0, 2, 1, 3) + tuple(range(4, split.ndim))
    flat = jnp.transpose(split, order).reshape((N_REFL * N_FREQ, across, along) + rest)
    flat = jnp.roll(flat, -2 * N_FREQ, axis=0)
    return flat.reshape((N_REFL, N_FREQ, across, along) + rest)

def reference(spectra, recorded, initial_filters):
    block_width = XR // N_REFL
    amplitude = 1.0 / math.sqrt(2.0 * XR)

    def add_block(block_index, carry):
        real_totals, imaginary_totals = carry
        first_point = (block_index * block_width).astype(jnp.int32)
        block_piece = lax.dynamic_slice_in_dim(spectra, first_point, block_width, 3).astype(jnp.float32)
        real_full = block_piece[0]
        imaginary_full = block_piece[1]
        real_source_rows = real_full[:, :NS]
        imaginary_source_rows = imaginary_full[:, :NS]
        real_portion = jnp.einsum('hvt,hkt->hvk', real_source_rows, real_full) - jnp.einsum('hvt,hkt->hvk', imaginary_source_rows, imaginary_full)
        imaginary_portion = jnp.einsum('hvt,hkt->hvk', real_source_rows, imaginary_full) + jnp.einsum('hvt,hkt->hvk', imaginary_source_rows, real_full)
        rounded_real = lax.optimization_barrier((amplitude * real_portion).astype(jnp.bfloat16))
        rounded_imag = lax.optimization_barrier((amplitude * imaginary_portion).astype(jnp.bfloat16))
        return (real_totals + rounded_real.astype(jnp.float32), imaginary_totals + rounded_imag.astype(jnp.float32))
    zeros_start = jnp.zeros((NF, NS, NR), jnp.float32)
    real_totals, imaginary_totals = lax.fori_loop(0, N_REFL, add_block, (zeros_start, zeros_start))
    spectrum = jnp.stack([real_totals, imaginary_totals]).astype(jnp.bfloat16)
    multiples = jnp.einsum('afsr,fat->srt', spectrum.astype(jnp.float32), time_table().astype(jnp.float32)).astype(jnp.bfloat16)
    recorded_grid = to_grid(recorded)
    start_grid = to_grid(initial_filters)
    support_width = WC + 2 * WM
    pad_width = ((WM, WM), (WM, WM), (0, 0))
    padded_multiples = jnp.pad(multiples, pad_width)
    padded_recorded = jnp.pad(recorded_grid, pad_width)
    wins_rows = NS // WC
    wins_cols = NR // WC

    def one_window(window_index):
        row_index = window_index // wins_cols
        column_index = window_index % wins_cols
        row_start = (row_index * WC).astype(jnp.int32)
        column_start = (column_index * WC).astype(jnp.int32)
        zero_start = jnp.zeros((), jnp.int32)
        support_multiples = lax.dynamic_slice(padded_multiples, (row_start, column_start, zero_start), (support_width, support_width, NT)).reshape(support_width * support_width, NT)
        support_recorded = lax.dynamic_slice(padded_recorded, (row_start, column_start, zero_start), (support_width, support_width, NT)).reshape(support_width * support_width, NT)
        gram_sums = jnp.dot(support_multiples.T, support_multiples, preferred_element_type=jnp.float32)
        cross_sums = jnp.dot(support_recorded.T, support_multiples, preferred_element_type=jnp.float32)
        filters = solve_filters(gram_sums, cross_sums, start_grid[row_index, column_index])
        core_multiples = lax.dynamic_slice(padded_multiples, (row_start + WM, column_start + WM, zero_start), (WC, WC, NT)).reshape(WC * WC, NT)
        core_recorded = lax.dynamic_slice(padded_recorded, (row_start + WM, column_start + WM, zero_start), (WC, WC, NT)).reshape(WC * WC, NT)
        predicted = jnp.dot(core_multiples, conv_matrix(filters.astype(jnp.bfloat16)), preferred_element_type=jnp.float32)
        cleaned = (core_recorded.astype(jnp.float32) - predicted).astype(jnp.bfloat16).reshape(WC, WC, NT)
        return (filters, cleaned)
    filters_all, cleaned_all = lax.map(one_window, jnp.arange(wins_rows * wins_cols, dtype=jnp.int32))
    cleaned_grid = jnp.transpose(cleaned_all.reshape(wins_rows, wins_cols, WC, WC, NT), (0, 2, 1, 3, 4)).reshape(NS, NR, NT)
    primaries = from_grid(cleaned_grid, TS, TR)
    filters_out = from_grid(filters_all.reshape(wins_rows, wins_cols, TAPS), TS // WC, TR // WC)
    return (primaries, filters_out)
```

```python
import functools
import math

import jax
import jax.numpy as jnp
import numpy as np
from jax import lax
from jax.experimental import pallas as pl
from jax.experimental.pallas import tpu as pltpu
from jax.sharding import PartitionSpec as P

NF = 16
K0 = 48
NT = 256
XR = 8192
WC = 32
WM = 4
TAPS = 33
ITERS = 3
HALF = (TAPS - 1) // 2
COLS = 4
LANES = 128
HF = 8
EXACT = lax.Precision.HIGHEST
F32 = jnp.float32
BF16 = jnp.bfloat16
VMEM = pltpu.CompilerParams(vmem_limit_bytes=32 * 1024 * 1024)


def tables():
    f = np.arange(NF)
    t = np.arange(NT)
    w = 2.0 * np.pi * (K0 + f) / NT
    angle = 2.0 * np.pi * (((K0 + f)[:, None] * t[None, :]) % NT) / NT
    weight = math.sqrt(2.0 / NF)
    table = np.stack([weight * np.cos(angle), -weight * np.sin(angle)], 1)
    table = table.astype(np.float32).astype(jnp.bfloat16).astype(np.float32)
    halves = table.reshape(2, HF, 2, NT).transpose(0, 2, 1, 3)
    time = halves.reshape(2, 2 * HF, NT)
    turned = np.stack([-halves[:, 1], halves[:, 0]], 1).reshape(2, 2 * HF, NT)
    lane = np.arange(LANES)
    held = lane < TAPS
    tap = lane - HALF
    cos_k = np.where(held, np.cos(w[:, None] * tap), 0.0).reshape(2, HF, LANES)
    sin_k = np.where(held, np.sin(w[:, None] * tap), 0.0).reshape(2, HF, LANES)
    lag = np.where(held, 16.0 * np.cos(w[:, None] * lane), 0.0).reshape(2, HF, LANES)
    zero = np.zeros_like(lag)
    to_lag = np.concatenate([lag, zero, zero, zero], 1)
    to_target = np.concatenate([zero, cos_k, sin_k, zero], 1)
    lags = np.concatenate([to_lag, to_target], 2)
    cos_rows = np.concatenate([cos_k, cos_k], 1)
    sin_rows = np.concatenate([sin_k, sin_k], 1)
    as32 = lambda x: np.asarray(x, np.float32)
    return time, as32(turned), as32(lags), as32(cos_rows), as32(sin_rows)


def lanes_of(rows):
    return lax.broadcasted_iota(jnp.int32, (rows, LANES), 1)


def band_rows(p, rows):
    if rows == 2:
        return [WC if p == 0 else WC - WM]
    return [p * WC - WM if p > 0 else None, (p + 1) * WC if p < rows - 1 else None]


def terms_kernel(rows, s_ref, *rest):
    refl = rows * COLS
    outs, (blocks, bands, sides) = rest[:refl], rest[refl:]
    f = pl.program_id(0)
    sources = rows * WC
    width = s_ref.shape[-1]
    amplitude = 1.0 / math.sqrt(2.0 * XR)
    left = s_ref[:, 0, :sources, :].reshape(2 * sources, width)
    parts = [[], []]
    for c in range(COLS):
        right = s_ref[:, 0, c * LANES : (c + 1) * LANES, :].reshape(2 * LANES, width)
        got = lax.dot_general(left, right, (((1,), (1,)), ((), ())), preferred_element_type=F32)
        parts[0].append(amplitude * (got[:sources, :LANES] - got[sources:, LANES:]))
        parts[1].append(amplitude * (got[:sources, LANES:] + got[sources:, :LANES]))
    low = lanes_of(WC // 2) < LANES // 2
    nb = len(band_rows(0, rows))
    for c in range(COLS):
        for p in range(rows):
            g = p * COLS + c
            for part in range(2):
                x = parts[part][c][p * WC : (p + 1) * WC]
                a, b = x[: WC // 2], x[WC // 2 :]
                first = jnp.where(low, a, pltpu.roll(b, LANES // 2, 1))
                second = jnp.where(low, pltpu.roll(a, LANES // 2, 1), b)
                at = pl.multiple_of(part * HF * WC + f * WC, WC)
                blocks[g, pl.ds(at, WC), :] = jnp.concatenate([first, second], 0).astype(BF16)
            for n, start in enumerate(band_rows(p, rows)):
                if start is None:
                    band = jnp.zeros((2 * WM, LANES), F32)
                else:
                    band = jnp.concatenate([x[c][start : start + WM] for x in parts], 0)
                bands[g, pl.ds(pl.multiple_of(n * HF * 8 + f * 8, 8), 8), :] = band
    lane = lanes_of(sources)
    zero = jnp.zeros((sources, LANES), F32)
    for c in range(COLS):
        for part in range(2):
            x = parts[part]
            before = x[c - 1] if c > 0 else zero
            after = x[c + 1] if c < COLS - 1 else zero
            base = f * 16 + part * 8
            moved = pltpu.roll(jnp.where(lane >= LANES // 2, before, after), base + WM, 1)
            here = (lane >= base) & (lane < base + 8)
            sides[c] = jnp.where(here, moved, sides[c])

    @pl.when(f == HF - 1)
    def _():
        me = lax.axis_index("refl")
        main = 2 * HF * WC
        for p in range(rows):
            for c in range(COLS):
                g = p * COLS + c
                blocks[g, main : main + nb * 64, :] = bands[g].astype(BF16)
                side = [sides[c, p * WC : (p + 1) * WC, :]]
                for start in band_rows(p, rows):
                    side.append(
                        jnp.zeros((WM, LANES), F32)
                        if start is None
                        else sides[c, start : start + WM, :]
                    )
                side.append(jnp.zeros((16 - nb * WM, LANES), F32))
                blocks[g, main + nb * 64 :, :] = jnp.concatenate(side, 0).astype(BF16)
        for k in range(refl):
            outs[k][...] = blocks[((me ^ k) + 2) % refl]


def block_terms(spectra, rows):
    refl = rows * COLS
    freqs, receivers, width = spectra.shape[1:]
    nb = len(band_rows(0, rows))
    size = 2 * HF * WC + nb * 64 + 48
    out = jax.ShapeDtypeStruct((size, LANES), BF16)
    spec = pl.BlockSpec((size, LANES), lambda f: (0, 0))
    return pl.pallas_call(
        functools.partial(terms_kernel, rows),
        grid=(freqs,),
        in_specs=[pl.BlockSpec((2, 1, receivers, width), lambda f: (0, f, 0, 0))],
        out_specs=[spec] * refl,
        out_shape=[out] * refl,
        scratch_shapes=[
            pltpu.VMEM((refl, size, LANES), BF16),
            pltpu.VMEM((refl, nb * 64, LANES), F32),
            pltpu.VMEM((COLS, rows * WC, LANES), F32),
        ],
        compiler_params=VMEM,
        name="block_terms",
    )(spectra)


def project_kernel(r_ref, t_ref, keep_ref, send_ref):
    j = lax.axis_index("freq")
    table = jnp.concatenate([t_ref[j], t_ref[1 - j]], 0)
    half = WC // 2
    for s in range(half):
        pair = jnp.concatenate([r_ref[s], r_ref[half + s]], 0)
        got = lax.dot_general(table, pair, (((1,), (1,)), ((), ())), preferred_element_type=F32)
        keep_ref[s] = got[: 2 * HF]
        send_ref[s] = got[2 * HF :]


def project(recorded, table):
    shape = jax.ShapeDtypeStruct((WC // 2, 2 * HF, LANES), F32)
    return pl.pallas_call(
        project_kernel, out_shape=[shape, shape], compiler_params=VMEM, name="project"
    )(recorded, table)


def grid_place(rows):
    g = (lax.axis_index("refl") + 2) % (rows * COLS)
    return g // COLS, g % COLS


def band_kernel(rows, keep_ref, other_ref, *outs):
    j = lax.axis_index("freq")
    p, _ = grid_place(rows)
    half = WC // 2
    low = lanes_of(HF) < LANES // 2

    def build(out_ref, first, upper):
        for s in range(WM):
            for part in range(2):
                rows_of = pl.ds(part * HF, HF)
                kept = keep_ref[first + s, rows_of, :]
                other = other_ref[first + s, rows_of, :]
                a = jnp.where(j == 0, kept, other)
                b = jnp.where(j == 0, other, kept)
                plain = jnp.where(low, a, pltpu.roll(b, LANES // 2, 1))
                shifted = jnp.where(low, pltpu.roll(a, LANES // 2, 1), b)
                band = jnp.where(upper, shifted, plain)
                out_ref[pl.ds(part * WM + s, HF, stride=8), :] = band

    if rows == 2:
        build(outs[0], jnp.where(p == 0, half - WM, 0), p == 0)
    else:
        build(outs[0], half - WM, True)
        build(outs[1], 0, False)


def band_projections(keep, other, rows):
    shape = jax.ShapeDtypeStruct((64, LANES), F32)
    return pl.pallas_call(
        functools.partial(band_kernel, rows),
        out_shape=[shape] * len(band_rows(0, rows)),
        name="band_projections",
    )(keep, other)


def side_kernel(keep_ref, other_ref, *rest):
    bands, out_ref = rest[:-1], rest[-1]
    j = lax.axis_index("freq")
    half = WC // 2
    keep = keep_ref[...].reshape(half * 2 * HF, LANES)
    other = other_ref[...].reshape(half * 2 * HF, LANES)
    left = jnp.where(j == 0, keep, other)
    right = jnp.where(j == 0, other, keep)
    row = lax.broadcasted_iota(jnp.int32, (LANES, LANES), 0)
    lane = lax.broadcasted_iota(jnp.int32, (LANES, LANES), 1)
    r = lane % 8
    dot = functools.partial(jnp.dot, precision=EXACT, preferred_element_type=F32)

    def picked(at_left, at_right):
        take_right = ((row == at_right + r) & (r < WM)).astype(F32)
        take_left = ((row == at_left + r - WM) & (r >= WM)).astype(F32)
        return take_left, take_right

    at = lax.broadcasted_iota(jnp.int32, (half, 2 * HF, LANES), 1)
    l3 = lax.broadcasted_iota(jnp.int32, (half, 2 * HF, LANES), 2)
    mine = (l3 // 16 == at % HF) & ((l3 // 8) % 2 == at // HF)
    for sh in range(2):
        take_left, take_right = picked(sh * 64, sh * 64 + 60)
        x = (dot(left, take_left) + dot(right, take_right)).reshape(half, 2 * HF, LANES)
        out_ref[sh * half : (sh + 1) * half, :] = jnp.sum(jnp.where(mine, x, 0.0), 1)
    take_left, take_right = picked(0, LANES - WM)
    b_row = lax.broadcasted_iota(jnp.int32, (HF, 8, LANES), 1)
    b_f = lax.broadcasted_iota(jnp.int32, (HF, 8, LANES), 0)
    b_l = lax.broadcasted_iota(jnp.int32, (HF, 8, LANES), 2)
    mine = (b_l // 16 == b_f) & ((b_l // 8) % 2 == b_row // WM)
    out_ref[WC:, :] = jnp.zeros((16, LANES), F32)
    for n, band in enumerate(bands):
        x = dot(band[...], take_left + take_right).reshape(HF, 8, LANES)
        x = jnp.sum(jnp.where(mine, x, 0.0), 0)
        out_ref[WC + n * WM : WC + (n + 1) * WM, :] = x[:WM] + x[WM:]


def side_projections(keep, other, bands):
    return pl.pallas_call(
        side_kernel,
        out_shape=jax.ShapeDtypeStruct((48, LANES), F32),
        name="side_projections",
    )(keep, other, *bands)


def statistics_kernel(rows, *refs):
    refl = rows * COLS
    nb = len(band_rows(0, rows))
    blocks, refs = refs[:refl], refs[refl:]
    keep_ref, other_ref, near_ref, far_ref, lags_ref = refs[:5]
    bands, refs = refs[5 : 5 + nb], refs[5 + nb :]
    own_ref, send_ref, lag_ref, spectrum = refs
    j = lax.axis_index("freq")
    _, c = grid_place(rows)
    half = WC // 2

    def summed(start, size):
        total = blocks[0][start : start + size, :].astype(F32)
        for block in blocks[1:]:
            total = total + block[start : start + size, :].astype(F32)
        return total.astype(BF16).astype(F32)

    for fp in range(2 * HF):
        x = summed(fp * WC, WC)
        for tile in range(2):
            spectrum[pl.ds(tile * half * 16 + fp, half, stride=16), :] = x[
                tile * half : (tile + 1) * half
            ]
    count = half * 16
    here = pl.multiple_of(j * count, count)
    there = pl.multiple_of((1 - j) * count, count)
    own_ref[...] = spectrum[pl.ds(here, count), :].astype(BF16)
    send_ref[...] = spectrum[pl.ds(there, count), :].astype(BF16)
    sums = []
    for at, q_ref in ((here, keep_ref), (there, other_ref)):
        power = in_phase = turned = jnp.zeros((HF, LANES), F32)
        for s in range(half):
            a = spectrum[pl.ds(at + s * 16, HF), :]
            b = spectrum[pl.ds(at + s * 16 + HF, HF), :]
            qc, qs = q_ref[s, :HF, :], q_ref[s, HF:, :]
            power = power + (a * a + b * b)
            in_phase = in_phase + (a * qc + b * qs)
            turned = turned + (b * qc - a * qs)
        sums.append([power, in_phase, turned])
    total = None
    sub = lax.broadcasted_iota(jnp.int32, (HF, 8, LANES), 1)
    for n in range(nb):
        x = summed(2 * HF * WC + n * 64, 64).reshape(HF, 8, LANES)
        q = bands[n][...].reshape(HF, 8, LANES)
        partner = jnp.where(sub < WM, -1.0, 1.0) * pltpu.roll(q, WM, 1)
        here_sums = [jnp.sum(x * y, 1) for y in (x, q, partner)]
        total = here_sums if total is None else [a + b for a, b in zip(total, here_sums)]
    sums.append(total)

    window = lax.broadcasted_iota(jnp.int32, (8, LANES), 0)
    lane = lanes_of(8)
    window = jnp.where(window < 4, (window + 2 * j) % 4, 8)
    starts = window * WC - WM

    def mask(receiver):
        return ((receiver >= starts) & (receiver < starts + WC + 2 * WM)).astype(F32)

    dot = functools.partial(lax.dot_general, precision=EXACT, preferred_element_type=F32)
    stats = jnp.zeros((8, 32), F32)
    receivers = (j * 64 + lane % 64, (1 - j) * 64 + lane % 64, lane)
    for x, receiver in zip(sums, receivers):
        x = jnp.concatenate(x + [jnp.zeros((HF, LANES), F32)], 0)
        stats = stats + dot(mask(receiver), x, (((1,), (1,)), ((), ())))
    x = summed(2 * HF * WC + nb * 64, 48)
    l48 = lanes_of(48)
    from_near = ((l48 % 8) < WM) == ((c % 2) == 1)
    q = jnp.where(from_near, near_ref[...], far_ref[...])
    first_part = (l48 // 8) % 2 == 0
    partner = jnp.where(first_part, -pltpu.roll(q, LANES - 8, 1), pltpu.roll(q, 8, 1))
    row = lax.broadcasted_iota(jnp.int32, (LANES, 32), 0)
    column = lax.broadcasted_iota(jnp.int32, (LANES, 32), 1)
    at_side = ((window == 0) & (lane % 8 < WM)) | ((window == 3) & (lane % 8 >= WM))
    for n, y in enumerate((x, q, partner)):
        z = jnp.sum(x * y, 0, keepdims=True)
        z = jnp.where(at_side, jnp.broadcast_to(z, (8, LANES)), 0.0)
        to = (column == n * HF + row // 16).astype(F32)
        stats = stats + dot(z, to, (((1,), (0,)), ((), ())))
    lag_ref[...] = dot(stats, lags_ref[j], (((1,), (0,)), ((), ())))


def statistics(blocks, keep, other, near, far, lags, bands, rows):
    count = WC // 2 * 2 * HF
    return pl.pallas_call(
        functools.partial(statistics_kernel, rows),
        out_shape=[
            jax.ShapeDtypeStruct((count, LANES), BF16),
            jax.ShapeDtypeStruct((count, LANES), BF16),
            jax.ShapeDtypeStruct((8, 2 * LANES), F32),
        ],
        scratch_shapes=[pltpu.VMEM((2 * count, LANES), F32)],
        compiler_params=VMEM,
        name="statistics",
    )(*blocks, keep, other, near, far, lags, *bands)


def subtract_kernel(
    steps,
    lag_ref,
    lag_got_ref,
    start_ref,
    time_ref,
    turned_ref,
    cos_ref,
    sin_ref,
    own_ref,
    got_ref,
    r_low_ref,
    r_high_ref,
    clean_ref,
    filters_ref,
    wavelets,
):
    step = pl.program_id(0)
    j = lax.axis_index("freq")
    half = WC // 2

    @pl.when(step == 0)
    def _():
        total = lag_ref[0:2, :] + lag_got_ref[2:4, :]
        lag, target = total[:, :LANES], total[:, LANES:]
        lane = lanes_of(2)
        held = lane < TAPS
        magnitude = jnp.where(held, jnp.abs(lag), 0.0)
        zero_lag = jnp.sum(jnp.where(lane == 0, lag, 0.0), 1, keepdims=True)
        others = jnp.sum(jnp.where(lane >= 1, magnitude, 0.0), 1, keepdims=True)
        step_size = 0.5 / (zero_lag + 2.0 * others + 1e-06)
        filters = jnp.concatenate(
            [start_ref[...], jnp.zeros((2, LANES - TAPS), F32)], 1
        )
        spread = [jnp.broadcast_to(lag[:, d : d + 1], (2, LANES)) for d in range(TAPS)]
        for repeat in range(ITERS):
            applied = spread[0] * filters
            for d in range(1, TAPS):
                applied = applied + spread[d] * (
                    pltpu.roll(filters, d, 1) + pltpu.roll(filters, LANES - d, 1)
                )
            filters = jnp.where(held, filters + step_size * (target - applied), 0.0)
        filters_ref[...] = filters[:, :TAPS]
        taps = filters.astype(BF16).astype(F32)
        for w in range(2):
            for n, h in enumerate((j, 1 - j)):
                tap = taps[w : w + 1, :]
                hc = jnp.sum(cos_ref[h] * tap, 1, keepdims=True)
                hs = jnp.sum(sin_ref[h] * tap, 1, keepdims=True)
                at = w * 32 + n * 16
                wavelets[at : at + 16, :] = (hc * time_ref[h] + hs * turned_ref[h]).astype(BF16)

    table = wavelets[...]
    lane = lax.broadcasted_iota(jnp.int32, (32, LANES), 1)
    first = (lane % 64) < WC
    zero = jnp.zeros((32, LANES), BF16)
    for s in range(half // steps):
        x = jnp.concatenate([own_ref[s * 16 : s * 16 + 16, :], got_ref[s * 16 : s * 16 + 16, :]], 0)
        both = jnp.concatenate([jnp.where(first, x, zero), jnp.where(first, zero, x)], 0)
        predicted = lax.dot_general(
            both, table, (((0,), (0,)), ((), ())), preferred_element_type=F32
        )
        clean_ref[0, s] = (r_low_ref[0, s].astype(F32) - predicted[:64]).astype(BF16)
        clean_ref[1, s] = (r_high_ref[0, s].astype(F32) - predicted[64:]).astype(BF16)


def subtract(lag, lag_got, start, time, turned, cos_rows, sin_rows, own, got, recorded):
    steps = 4
    half = WC // 2
    each = half // steps
    recorded = recorded.reshape(2, half, 64, NT)
    whole = lambda x: pl.BlockSpec(x.shape, lambda i: (0,) * x.ndim)
    small = (lag, lag_got, start, time, turned, cos_rows, sin_rows)
    rows_spec = pl.BlockSpec((each * 16, LANES), lambda i: (i, 0))
    return pl.pallas_call(
        functools.partial(subtract_kernel, steps),
        grid=(steps,),
        in_specs=[whole(x) for x in small]
        + [
            rows_spec,
            rows_spec,
            pl.BlockSpec((1, each, 64, NT), lambda i: (0, i, 0, 0)),
            pl.BlockSpec((1, each, 64, NT), lambda i: (1, i, 0, 0)),
        ],
        out_specs=[
            pl.BlockSpec((2, each, 64, NT), lambda i: (0, i, 0, 0)),
            pl.BlockSpec((2, TAPS), lambda i: (0, 0)),
        ],
        out_shape=[
            jax.ShapeDtypeStruct((2, half, 64, NT), BF16),
            jax.ShapeDtypeStruct((2, TAPS), F32),
        ],
        scratch_shapes=[pltpu.VMEM((64, NT), BF16)],
        compiler_params=VMEM,
        name="subtract",
    )(*small, own, got, recorded, recorded)


def body(spectra, recorded, initial_filters):
    refl = lax.axis_size("refl")
    rows = refl // COLS
    time, turned, lags, cos_rows, sin_rows = (jnp.asarray(x) for x in tables())
    core_swap = [(0, 1), (1, 0)]

    def place(p, c):
        return (p * COLS + c - 2) % refl

    blocks = block_terms(spectra, rows)
    got = [blocks[0]]
    for k in range(1, refl):
        got.append(lax.ppermute(blocks[k], "refl", [(i, i ^ k) for i in range(refl)]))

    tile = recorded[0, 0]
    keep, send = project(tile, time.astype(BF16))
    other = lax.ppermute(send, "freq", core_swap)
    bands = band_projections(keep, other, rows)
    if rows == 2:
        routes = [[(place(p, c), place(1 - p, c)) for p in range(2) for c in range(COLS)]]
    else:
        routes = [
            [(place(p, c), place(p + 1, c)) for p in range(rows - 1) for c in range(COLS)],
            [(place(p + 1, c), place(p, c)) for p in range(rows - 1) for c in range(COLS)],
        ]
    bands = [lax.ppermute(x, "refl", route) for x, route in zip(bands, routes)]
    sides = side_projections(keep, other, bands)
    near = lax.ppermute(
        sides, "refl", [(place(p, c), place(p, c ^ 1)) for p in range(rows) for c in range(COLS)]
    )
    far = lax.ppermute(
        sides, "refl", [(place(p, c), place(p, 3 - c)) for p in range(rows) for c in (1, 2)]
    )
    own, away, lag = statistics(got, keep, other, near, far, lags, bands, rows)
    came = lax.ppermute(away, "freq", core_swap)
    lag_got = lax.ppermute(lag, "freq", core_swap)
    clean, filters = subtract(
        lag,
        lag_got,
        initial_filters.reshape(2, TAPS),
        time,
        turned,
        cos_rows,
        sin_rows,
        own,
        came,
        tile,
    )
    return (clean.reshape(recorded.shape), filters.reshape(initial_filters.shape))


def solution(mesh):
    placed = (
        P(None, "freq", "groups", "refl"),
        P("refl", "freq", "groups", None, None),
        P("refl", "freq", "groups", None, None),
    )
    return jax.shard_map(
        body,
        mesh=mesh,
        in_specs=placed,
        out_specs=(
            P("refl", "freq", "groups", None, None),
            P("refl", "freq", "groups", None, None),
        ),
        check_vma=False,
    )
```

```python
import functools
import math

import jax
import jax.numpy as jnp
import numpy as np
from jax import lax
from jax.experimental import pallas as pl
from jax.experimental.pallas import tpu as pltpu
from jax.sharding import PartitionSpec as P

NF = 16
K0 = 48
NT = 256
XR = 8192
WC = 32
WM = 4
TAPS = 33
ITERS = 3
HALF = (TAPS - 1) // 2
COLS = 4
LANES = 128
HF = 8
TERMS_VMEM = 48 * 1024 * 1024
AHEAD = 3
EXACT = lax.Precision.HIGHEST
F32 = jnp.float32
BF16 = jnp.bfloat16
VMEM = pltpu.CompilerParams(vmem_limit_bytes=12 * 1024 * 1024)


def tables():
    f = np.arange(NF)
    t = np.arange(NT)
    w = 2.0 * np.pi * (K0 + f) / NT
    angle = 2.0 * np.pi * (((K0 + f)[:, None] * t[None, :]) % NT) / NT
    weight = math.sqrt(2.0 / NF)
    table = np.stack([weight * np.cos(angle), -weight * np.sin(angle)], 1)
    table = table.astype(np.float32).astype(jnp.bfloat16).astype(np.float32)
    halves = table.reshape(2, HF, 2, NT).transpose(0, 2, 1, 3)
    time = halves.reshape(2, 2 * HF, NT)
    turned = np.stack([-halves[:, 1], halves[:, 0]], 1).reshape(2, 2 * HF, NT)
    lane = np.arange(LANES)
    held = lane < TAPS
    tap = lane - HALF
    cos_k = np.where(held, np.cos(w[:, None] * tap), 0.0).reshape(2, HF, LANES)
    sin_k = np.where(held, np.sin(w[:, None] * tap), 0.0).reshape(2, HF, LANES)
    lag = np.where(held, 16.0 * np.cos(w[:, None] * lane), 0.0).reshape(2, HF, LANES)
    zero = np.zeros_like(lag)
    to_lag = np.concatenate([lag, zero, zero, zero], 1)
    to_target = np.concatenate([zero, cos_k, sin_k, zero], 1)
    lags = np.concatenate([to_lag, to_target], 2)
    trig = np.concatenate([np.concatenate([cos_k, cos_k], 1), np.concatenate([sin_k, sin_k], 1)], 2)
    return np.concatenate([time, turned, lags, trig], 1).astype(np.float32)


TIME, TURNED, LAGS, TRIG = (slice(0, 16), slice(16, 32), slice(32, 64), slice(64, 80))


def lanes_of(rows):
    return lax.broadcasted_iota(jnp.int32, (rows, LANES), 1)


def band_rows(p, rows):
    if rows == 2:
        return [WC if p == 0 else WC - WM]
    return [p * WC - WM if p > 0 else None, (p + 1) * WC if p < rows - 1 else None]


def terms_kernel(rows, s_hbm, *rest):
    refl = rows * COLS
    outs, (buffer, blocks, bands, sides, arrived) = rest[:-5], rest[-5:]
    sources = rows * WC
    freqs, _, _, width = buffer.shape
    amplitude = 1.0 / math.sqrt(2.0 * XR)
    nb = len(band_rows(0, rows))
    main = 2 * HF * WC

    def fetch(f, part):
        return pltpu.make_async_copy(s_hbm.at[part, f], buffer.at[f, part], arrived.at[f, part])

    for f in range(AHEAD):
        for part in range(2):
            fetch(f, part).start()

    def products(f):
        if f + AHEAD < freqs:
            for part in range(2):
                fetch(f + AHEAD, part).start()
        for part in range(2):
            fetch(f, part).wait()
        left = buffer[f, :, :sources, :].reshape(2 * sources, width)
        parts = [[], []]
        for c in range(COLS):
            right = buffer[f, :, c * LANES : (c + 1) * LANES, :].reshape(2 * LANES, width)
            got = lax.dot_general(left, right, (((1,), (1,)), ((), ())), preferred_element_type=F32)
            parts[0].append(amplitude * (got[:sources, :LANES] - got[sources:, LANES:]))
            parts[1].append(amplitude * (got[:sources, LANES:] + got[sources:, :LANES]))
        return parts

    def place(f, parts):
        for c in range(COLS):
            for p in range(rows):
                g = p * COLS + c
                for part in range(2):
                    at = part * HF * WC + f * WC
                    x = parts[part][c][p * WC : (p + 1) * WC]
                    blocks[g, at : at + WC, :] = x.astype(BF16)
                for n, start in enumerate(band_rows(p, rows)):
                    if start is None:
                        band = jnp.zeros((2 * WM, LANES), F32)
                    else:
                        band = jnp.concatenate([x[c][start : start + WM] for x in parts], 0)
                    bands[g, n * HF * 8 + f * 8 : n * HF * 8 + f * 8 + 8, :] = band
        lane = lanes_of(sources)
        base = f * 16
        first = (lane >= base) & (lane < base + 8)
        second = (lane >= base + 8) & (lane < base + 16)
        zero = jnp.zeros((sources, LANES), F32)
        for c in range(COLS):
            side = sides[c]
            for part, here in enumerate((first, second)):
                x = parts[part]
                before = x[c - 1] if c > 0 else zero
                after = x[c + 1] if c < COLS - 1 else zero
                moved = jnp.where(lane >= LANES // 2, before, after)
                moved = pltpu.roll(moved, (base + part * 8 + WM) % LANES, 1)
                side = jnp.where(here, moved, side)
            sides[c] = side

    before = None
    for f in range(freqs):
        parts = products(f)
        if before is not None:
            place(f - 1, before)
        before = parts
    place(freqs - 1, before)
    me = lax.axis_index("refl")
    for p in range(rows):
        for c in range(COLS):
            g = p * COLS + c
            blocks[g, main : main + nb * 64, :] = bands[g].astype(BF16)
            side = [sides[c, p * WC : (p + 1) * WC, :]]
            for start in band_rows(p, rows):
                side.append(
                    jnp.zeros((WM, LANES), F32)
                    if start is None
                    else sides[c, start : start + WM, :]
                )
            side.append(jnp.zeros((16 - nb * WM, LANES), F32))
            blocks[g, main + nb * 64 :, :] = jnp.concatenate(side, 0).astype(BF16)
    for out, k in zip(outs, parcels(refl)):
        out[...] = blocks[((me ^ k) + 2) % refl]


def parcels(refl):
    places = list(range(refl - 2, -1, -2))
    return [k ^ 1 for k in places] + places


def block_terms(spectra, rows):
    refl = rows * COLS
    freqs, receivers, width = spectra.shape[1:]
    nb = len(band_rows(0, rows))
    size = 2 * HF * WC + nb * 64 + 48
    return pl.pallas_call(
        functools.partial(terms_kernel, rows),
        in_specs=[pl.BlockSpec(memory_space=pl.ANY)],
        out_shape=[jax.ShapeDtypeStruct((size, LANES), BF16)] * refl,
        scratch_shapes=[
            pltpu.VMEM((freqs, 2, receivers, width), BF16),
            pltpu.VMEM((refl, size, LANES), BF16),
            pltpu.VMEM((refl, nb * 64, LANES), F32),
            pltpu.VMEM((COLS, rows * WC, LANES), F32),
            pltpu.SemaphoreType.DMA((freqs, 2)),
        ],
        compiler_params=pltpu.CompilerParams(vmem_limit_bytes=TERMS_VMEM),
        name="block_terms",
    )(spectra)


def project_kernel(r_ref, t_ref, keep_ref, send_ref):
    j = lax.axis_index("freq")
    table = jnp.concatenate([t_ref[j, TIME], t_ref[1 - j, TIME]], 0).astype(BF16)
    half = WC // 2
    for s in range(half):
        pair = jnp.concatenate([r_ref[s], r_ref[half + s]], 0)
        got = lax.dot_general(table, pair, (((1,), (1,)), ((), ())), preferred_element_type=F32)
        keep_ref[s] = got[: 2 * HF]
        send_ref[s] = got[2 * HF :]


def project(recorded, table):
    shape = jax.ShapeDtypeStruct((WC // 2, 2 * HF, LANES), F32)
    return pl.pallas_call(
        project_kernel, out_shape=[shape, shape], compiler_params=VMEM, name="project"
    )(recorded, table)


def grid_place(rows):
    g = (lax.axis_index("refl") + 2) % (rows * COLS)
    return g // COLS, g % COLS


def edge_kernel(rows, keep_ref, other_ref, *outs):
    bands, sides_ref = outs[:-1], outs[-1]
    j = lax.axis_index("freq")
    p, _ = grid_place(rows)
    half = WC // 2
    low = lanes_of(HF) < LANES // 2

    def build(out_ref, first, upper):
        for s in range(WM):
            for part in range(2):
                rows_of = pl.ds(part * HF, HF)
                kept = keep_ref[first + s, rows_of, :]
                other = other_ref[first + s, rows_of, :]
                a = jnp.where(j == 0, kept, other)
                b = jnp.where(j == 0, other, kept)
                plain = jnp.where(low, a, pltpu.roll(b, LANES // 2, 1))
                shifted = jnp.where(low, pltpu.roll(a, LANES // 2, 1), b)
                band = jnp.where(upper, shifted, plain)
                out_ref[pl.ds(part * WM + s, HF, stride=8), :] = band

    if rows == 2:
        build(bands[0], jnp.where(p == 0, half - WM, 0), p == 0)
    else:
        build(bands[0], half - WM, True)
        build(bands[1], 0, False)

    keep = keep_ref[...].reshape(half * 2 * HF, LANES)
    other = other_ref[...].reshape(half * 2 * HF, LANES)
    left = jnp.where(j == 0, keep, other).astype(BF16)
    right = jnp.where(j == 0, other, keep).astype(BF16)
    row = lax.broadcasted_iota(jnp.int32, (LANES, LANES), 0)
    r = lax.broadcasted_iota(jnp.int32, (LANES, LANES), 1) % 8
    at = lax.broadcasted_iota(jnp.int32, (half, 2 * HF, LANES), 1)
    lane = lax.broadcasted_iota(jnp.int32, (half, 2 * HF, LANES), 2)
    mine = (lane // 16 == at % HF) & ((lane // 8) % 2 == at // HF)
    for upper in range(2):
        from_right = ((row == upper * 64 + 60 + r) & (r < WM)).astype(F32).astype(BF16)
        from_left = ((row == upper * 64 + r - WM) & (r >= WM)).astype(F32).astype(BF16)
        x = jnp.dot(left, from_left, preferred_element_type=F32)
        x = x + jnp.dot(right, from_right, preferred_element_type=F32)
        x = jnp.where(mine, x.reshape(half, 2 * HF, LANES), 0.0)
        sides_ref[upper * half : (upper + 1) * half, :] = jnp.sum(x, 1)


def edge_projections(keep, other, rows):
    nb = len(band_rows(0, rows))
    return pl.pallas_call(
        functools.partial(edge_kernel, rows),
        out_shape=[jax.ShapeDtypeStruct((64, LANES), F32)] * nb
        + [jax.ShapeDtypeStruct((WC, LANES), F32)],
        compiler_params=VMEM,
        name="edge_projections",
    )(keep, other)


def statistics_kernel(rows, *refs):
    nb = len(band_rows(0, rows))
    count = rows * COLS // 2 + 1
    blocks, refs = refs[:count], refs[count:]
    keep_ref, other_ref, lags_ref = refs[:3]
    bands, refs = refs[3 : 3 + nb], refs[3 + nb :]
    nears, refs = refs[: 1 + nb], refs[1 + nb :]
    fars, refs = refs[: 1 + nb], refs[1 + nb :]
    own_ref, send_ref, lag_ref, spectrum = refs
    j = lax.axis_index("freq")
    p, c = grid_place(rows)
    half = WC // 2

    def summed(start, size):
        total = blocks[0][start : start + size, :].astype(F32)
        for block in blocks[1:]:
            total = total + block[start : start + size, :].astype(F32)
        return total.astype(BF16).astype(F32)

    low = lanes_of(half) < LANES // 2
    for fp in range(2 * HF):
        x = summed(fp * WC, WC)
        a, b = x[:half], x[half:]
        first = jnp.where(low, a, pltpu.roll(b, LANES // 2, 1))
        second = jnp.where(low, pltpu.roll(a, LANES // 2, 1), b)
        spectrum[pl.ds(fp, half, stride=16), :] = first
        spectrum[pl.ds(half * 16 + fp, half, stride=16), :] = second
    count = half * 16
    here = pl.multiple_of(j * count, count)
    there = pl.multiple_of((1 - j) * count, count)
    own_ref[...] = spectrum[pl.ds(here, count), :].astype(BF16)
    send_ref[...] = spectrum[pl.ds(there, count), :].astype(BF16)
    sums = []
    for at, q_ref in ((here, keep_ref), (there, other_ref)):
        power = in_phase = turned = jnp.zeros((HF, LANES), F32)
        for s in range(half):
            a = spectrum[pl.ds(at + s * 16, HF), :]
            b = spectrum[pl.ds(at + s * 16 + HF, HF), :]
            qc, qs = q_ref[s, :HF, :], q_ref[s, HF:, :]
            power = power + (a * a + b * b)
            in_phase = in_phase + (a * qc + b * qs)
            turned = turned + (b * qc - a * qs)
        sums.append([power, in_phase, turned])
    total = None
    sub = lax.broadcasted_iota(jnp.int32, (HF, 8, LANES), 1)
    for n in range(nb):
        x = summed(2 * HF * WC + n * 64, 64).reshape(HF, 8, LANES)
        q = bands[n][...].reshape(HF, 8, LANES)
        partner = jnp.where(sub < WM, -1.0, 1.0) * pltpu.roll(q, WM, 1)
        here_sums = [jnp.sum(x * y, 1) for y in (x, q, partner)]
        total = here_sums if total is None else [a + b for a, b in zip(total, here_sums)]
    sums.append(total)

    window = lax.broadcasted_iota(jnp.int32, (8, LANES), 0)
    lane = lanes_of(8)
    window = jnp.where(window < 4, (window + 2 * j) % 4, 8)
    starts = window * WC - WM

    def mask(receiver):
        return ((receiver >= starts) & (receiver < starts + WC + 2 * WM)).astype(F32)

    dot = functools.partial(lax.dot_general, precision=EXACT, preferred_element_type=F32)
    stats = jnp.zeros((8, 32), F32)
    receivers = (j * 64 + lane % 64, (1 - j) * 64 + lane % 64, lane)
    for x, receiver in zip(sums, receivers):
        x = jnp.concatenate(x + [jnp.zeros((HF, LANES), F32)], 0)
        stats = stats + dot(mask(receiver), x, (((1,), (1,)), ((), ())))
    x = summed(2 * HF * WC + nb * 64, 48)
    l48 = lanes_of(48)
    from_near = ((l48 % 8) < WM) == ((c % 2) == 1)
    q = []
    for sides in (nears, fars):
        pieces = [sides[0][...]]
        for n, side in enumerate(sides[1:]):
            top, bottom = side[:WM, :], side[WC - WM :, :]
            pieces.append(jnp.where(p == 0, top, bottom) if nb == 1 else (bottom, top)[n])
        pieces.append(jnp.zeros((16 - nb * WM, LANES), F32))
        q.append(jnp.concatenate(pieces, 0))
    q = jnp.where(from_near, q[0], q[1])
    first_part = (l48 // 8) % 2 == 0
    partner = jnp.where(first_part, -pltpu.roll(q, LANES - 8, 1), pltpu.roll(q, 8, 1))
    row = lax.broadcasted_iota(jnp.int32, (LANES, 32), 0)
    column = lax.broadcasted_iota(jnp.int32, (LANES, 32), 1)
    at_side = ((window == 0) & (lane % 8 < WM)) | ((window == 3) & (lane % 8 >= WM))
    for n, y in enumerate((x, q, partner)):
        z = jnp.sum(x * y, 0, keepdims=True)
        z = jnp.where(at_side, jnp.broadcast_to(z, (8, LANES)), 0.0)
        to = (column == n * HF + row // 16).astype(F32)
        stats = stats + dot(z, to, (((1,), (0,)), ((), ())))
    lag_ref[...] = dot(stats, lags_ref[j, LAGS], (((1,), (0,)), ((), ())))


def statistics(blocks, keep, other, table, bands, nears, fars, rows):
    count = WC // 2 * 2 * HF
    return pl.pallas_call(
        functools.partial(statistics_kernel, rows),
        out_shape=[
            jax.ShapeDtypeStruct((count, LANES), BF16),
            jax.ShapeDtypeStruct((count, LANES), BF16),
            jax.ShapeDtypeStruct((8, 2 * LANES), F32),
        ],
        scratch_shapes=[pltpu.VMEM((2 * count, LANES), F32)],
        compiler_params=VMEM,
        name="statistics",
    )(*blocks, keep, other, table, *bands, *nears, *fars)


def subtract_kernel(
    steps,
    lag_ref,
    lag_got_ref,
    start_ref,
    table_ref,
    own_ref,
    got_ref,
    r_low_ref,
    r_high_ref,
    clean_ref,
    filters_ref,
    wavelets,
):
    step = pl.program_id(0)
    j = lax.axis_index("freq")
    half = WC // 2

    @pl.when(step == 0)
    def _():
        total = lag_ref[0:2, :] + lag_got_ref[2:4, :]
        lag, target = total[:, :LANES], total[:, LANES:]
        lane = lanes_of(2)
        held = lane < TAPS
        magnitude = jnp.where(held, jnp.abs(lag), 0.0)
        zero_lag = jnp.sum(jnp.where(lane == 0, lag, 0.0), 1, keepdims=True)
        others = jnp.sum(jnp.where(lane >= 1, magnitude, 0.0), 1, keepdims=True)
        step_size = 0.5 / (zero_lag + 2.0 * others + 1e-06)
        filters = jnp.concatenate(
            [start_ref[...], jnp.zeros((2, LANES - TAPS), F32)], 1
        )
        spread = [jnp.broadcast_to(lag[:, d : d + 1], (2, LANES)) for d in range(TAPS)]
        for repeat in range(ITERS):
            applied = spread[0] * filters
            for d in range(1, TAPS):
                applied = applied + spread[d] * (
                    pltpu.roll(filters, d, 1) + pltpu.roll(filters, LANES - d, 1)
                )
            filters = jnp.where(held, filters + step_size * (target - applied), 0.0)
        filters_ref[...] = filters[:, :TAPS]
        taps = filters.astype(BF16).astype(F32)
        for w in range(2):
            for n, h in enumerate((j, 1 - j)):
                tap = taps[w : w + 1, :]
                hc = jnp.sum(table_ref[h, TRIG, :LANES] * tap, 1, keepdims=True)
                hs = jnp.sum(table_ref[h, TRIG, LANES:] * tap, 1, keepdims=True)
                wave = hc * table_ref[h, TIME] + hs * table_ref[h, TURNED]
                at = w * 32 + n * 16
                wavelets[at : at + 16, :] = wave.astype(BF16)

    table = wavelets[...]
    lane = lax.broadcasted_iota(jnp.int32, (32, LANES), 1)
    first = (lane % 64) < WC
    zero = jnp.zeros((32, LANES), BF16)
    for s in range(half // steps):
        x = jnp.concatenate([own_ref[s * 16 : s * 16 + 16, :], got_ref[s * 16 : s * 16 + 16, :]], 0)
        both = jnp.concatenate([jnp.where(first, x, zero), jnp.where(first, zero, x)], 0)
        predicted = lax.dot_general(
            both, table, (((0,), (0,)), ((), ())), preferred_element_type=F32
        )
        clean_ref[0, s] = (r_low_ref[0, s].astype(F32) - predicted[:64]).astype(BF16)
        clean_ref[1, s] = (r_high_ref[0, s].astype(F32) - predicted[64:]).astype(BF16)


def subtract(lag, lag_got, start, table, own, got, recorded):
    steps = 4
    half = WC // 2
    each = half // steps
    recorded = recorded.reshape(2, half, 64, NT)
    whole = lambda x: pl.BlockSpec(x.shape, lambda i: (0,) * x.ndim)
    small = (lag, lag_got, start, table)
    rows_spec = pl.BlockSpec((each * 16, LANES), lambda i: (i, 0))
    return pl.pallas_call(
        functools.partial(subtract_kernel, steps),
        grid=(steps,),
        in_specs=[whole(x) for x in small]
        + [
            rows_spec,
            rows_spec,
            pl.BlockSpec((1, each, 64, NT), lambda i: (0, i, 0, 0)),
            pl.BlockSpec((1, each, 64, NT), lambda i: (1, i, 0, 0)),
        ],
        out_specs=[
            pl.BlockSpec((2, each, 64, NT), lambda i: (0, i, 0, 0)),
            pl.BlockSpec((2, TAPS), lambda i: (0, 0)),
        ],
        out_shape=[
            jax.ShapeDtypeStruct((2, half, 64, NT), BF16),
            jax.ShapeDtypeStruct((2, TAPS), F32),
        ],
        scratch_shapes=[pltpu.VMEM((64, NT), BF16)],
        compiler_params=VMEM,
        name="subtract",
    )(*small, own, got, recorded, recorded)


def body(spectra, recorded, initial_filters):
    refl = lax.axis_size("refl")
    rows = refl // COLS
    table = jnp.asarray(tables())
    core_swap = [(0, 1), (1, 0)]

    def place(p, c):
        return (p * COLS + c - 2) % refl

    def swap(x, k):
        return lax.ppermute(x, "refl", [(i, i ^ k) for i in range(refl)])

    def add(x, y):
        return (x.astype(F32) + y.astype(F32)).astype(BF16)

    after = lax.optimization_barrier
    blocks = block_terms(spectra, rows)
    pairs = refl // 2
    sent, kept = list(blocks[:pairs]), blocks[pairs:]
    came = [swap(sent[0], 1)]
    tile, sent[1] = after((recorded[0, 0], sent[1]))
    keep, send = project(tile, table)
    other = lax.ppermute(send, "freq", core_swap)
    *bands, sides = edge_projections(keep, other, rows)
    sent[1], sides, *bands = after((sent[1], sides, *bands))
    came.append(swap(sent[1], 1))
    if rows == 2:
        near = swap(sides, 1)
    got = []
    for n, k in enumerate(range(refl - 2, 0, -2)):
        total = add(kept[n], came[n])
        if n + 2 < pairs:
            total, sent[n + 2] = after((total, sent[n + 2]))
            came.append(swap(sent[n + 2], 1))
        if rows == 2 and n == 0:
            total, near, bands[0] = after((total, near, bands[0]))
        came[n + 1], total = after((came[n + 1], total))
        got.append(swap(total, k))
        if rows == 2 and n == 1:
            bands = [swap(bands[0], k)]
    got = [kept[-1], came[-1]] + got
    if rows == 2:
        nears, fars = [near, swap(near, 4)], [swap(near, 6), swap(near, 2)]
    else:

        def shift(x, rise, across):
            route = [
                (place(p, c), place(p + rise, across[c]))
                for p in range(rows)
                for c in range(COLS)
                if 0 <= p + rise < rows and across[c] is not None
            ]
            return lax.ppermute(x, "refl", route)

        bands = [shift(x, rise, (0, 1, 2, 3)) for x, rise in zip(bands, (1, -1))]
        nears = [shift(sides, rise, (1, 0, 3, 2)) for rise in (0, 1, -1)]
        fars = [shift(sides, rise, (None, 2, 1, None)) for rise in (0, 1, -1)]
    own, away, lag = statistics(got, keep, other, table, bands, nears, fars, rows)
    away_got = lax.ppermute(away, "freq", core_swap)
    lag_got = lax.ppermute(lag, "freq", core_swap)
    clean, filters = subtract(
        lag,
        lag_got,
        initial_filters.reshape(2, TAPS),
        table,
        own,
        away_got,
        tile,
    )
    return (clean.reshape(recorded.shape), filters.reshape(initial_filters.shape))


def solution(mesh):
    placed = (
        P(None, "freq", "groups", "refl"),
        P("refl", "freq", "groups", None, None),
        P("refl", "freq", "groups", None, None),
    )
    return jax.shard_map(
        body,
        mesh=mesh,
        in_specs=placed,
        out_specs=(
            P("refl", "freq", "groups", None, None),
            P("refl", "freq", "groups", None, None),
        ),
        check_vma=False,
    )
```

```python
import functools
import math

import jax
import jax.numpy as jnp
import numpy as np
from jax import lax
from jax.experimental import pallas as pl
from jax.experimental.pallas import tpu as pltpu
from jax.sharding import PartitionSpec as P

NF = 16
K0 = 48
NT = 256
XR = 8192
WC = 32
WM = 4
TAPS = 33
ITERS = 3
HALF = (TAPS - 1) // 2
COLS = 4
LANES = 128
HF = 8
TERMS_VMEM = 48 * 1024 * 1024
AHEAD = 3
EXACT = lax.Precision.HIGHEST
F32 = jnp.float32
BF16 = jnp.bfloat16
VMEM = pltpu.CompilerParams(vmem_limit_bytes=12 * 1024 * 1024)


def tables():
    f = np.arange(NF)
    t = np.arange(NT)
    w = 2.0 * np.pi * (K0 + f) / NT
    angle = 2.0 * np.pi * (((K0 + f)[:, None] * t[None, :]) % NT) / NT
    weight = math.sqrt(2.0 / NF)
    table = np.stack([weight * np.cos(angle), -weight * np.sin(angle)], 1)
    table = table.astype(np.float32).astype(jnp.bfloat16).astype(np.float32)
    halves = table.reshape(2, HF, 2, NT).transpose(0, 2, 1, 3)
    time = halves.reshape(2, 2 * HF, NT)
    turned = np.stack([-halves[:, 1], halves[:, 0]], 1).reshape(2, 2 * HF, NT)
    lane = np.arange(LANES)
    held = lane < TAPS
    tap = lane - HALF
    cos_k = np.where(held, np.cos(w[:, None] * tap), 0.0).reshape(2, HF, LANES)
    sin_k = np.where(held, np.sin(w[:, None] * tap), 0.0).reshape(2, HF, LANES)
    lag = np.where(held, 16.0 * np.cos(w[:, None] * lane), 0.0).reshape(2, HF, LANES)
    zero = np.zeros_like(lag)
    to_lag = np.concatenate([lag, zero, zero, zero], 1)
    to_target = np.concatenate([zero, cos_k, sin_k, zero], 1)
    lags = np.concatenate([to_lag, to_target], 2)
    trig = np.concatenate([np.concatenate([cos_k, cos_k], 1), np.concatenate([sin_k, sin_k], 1)], 2)
    return np.concatenate([time, turned, lags, trig], 1).astype(np.float32)


TIME, TURNED, LAGS, TRIG = (slice(0, 16), slice(16, 32), slice(32, 64), slice(64, 80))


def lanes_of(rows):
    return lax.broadcasted_iota(jnp.int32, (rows, LANES), 1)


def band_rows(p, rows):
    if rows == 2:
        return [WC if p == 0 else WC - WM]
    return [p * WC - WM if p > 0 else None, (p + 1) * WC if p < rows - 1 else None]


def terms_kernel(rows, s_hbm, *rest):
    refl = rows * COLS
    outs, (buffer, blocks, bands, sides, arrived) = rest[:-5], rest[-5:]
    sources = rows * WC
    freqs, _, _, width = buffer.shape
    amplitude = 1.0 / math.sqrt(2.0 * XR)
    nb = len(band_rows(0, rows))
    main = 2 * HF * WC

    def fetch(f, part):
        return pltpu.make_async_copy(s_hbm.at[part, f], buffer.at[f, part], arrived.at[f, part])

    for f in range(AHEAD):
        for part in range(2):
            fetch(f, part).start()

    def products(f):
        if f + AHEAD < freqs:
            for part in range(2):
                fetch(f + AHEAD, part).start()
        for part in range(2):
            fetch(f, part).wait()
        left = buffer[f, :, :sources, :].reshape(2 * sources, width)
        parts = [[], []]
        for c in range(COLS):
            right = buffer[f, :, c * LANES : (c + 1) * LANES, :].reshape(2 * LANES, width)
            got = lax.dot_general(left, right, (((1,), (1,)), ((), ())), preferred_element_type=F32)
            parts[0].append(amplitude * (got[:sources, :LANES] - got[sources:, LANES:]))
            parts[1].append(amplitude * (got[:sources, LANES:] + got[sources:, :LANES]))
        return parts

    def place(f, parts):
        for c in range(COLS):
            for p in range(rows):
                g = p * COLS + c
                for part in range(2):
                    at = part * HF * WC + f * WC
                    x = parts[part][c][p * WC : (p + 1) * WC]
                    blocks[g, at : at + WC, :] = x.astype(BF16)
                for n, start in enumerate(band_rows(p, rows)):
                    if start is None:
                        band = jnp.zeros((2 * WM, LANES), F32)
                    else:
                        band = jnp.concatenate([x[c][start : start + WM] for x in parts], 0)
                    bands[g, n * HF * 8 + f * 8 : n * HF * 8 + f * 8 + 8, :] = band
        lane = lanes_of(sources)
        base = f * 16
        first = (lane >= base) & (lane < base + 8)
        second = (lane >= base + 8) & (lane < base + 16)
        zero = jnp.zeros((sources, LANES), F32)
        for c in range(COLS):
            side = sides[c]
            for part, here in enumerate((first, second)):
                x = parts[part]
                before = x[c - 1] if c > 0 else zero
                after = x[c + 1] if c < COLS - 1 else zero
                moved = jnp.where(lane >= LANES // 2, before, after)
                moved = pltpu.roll(moved, (base + part * 8 + WM) % LANES, 1)
                side = jnp.where(here, moved, side)
            sides[c] = side

    before = None
    for f in range(freqs):
        parts = products(f)
        if before is not None:
            place(f - 1, before)
        before = parts
    place(freqs - 1, before)
    me = lax.axis_index("refl")
    for p in range(rows):
        for c in range(COLS):
            g = p * COLS + c
            blocks[g, main : main + nb * 64, :] = bands[g].astype(BF16)
            side = [sides[c, p * WC : (p + 1) * WC, :]]
            for start in band_rows(p, rows):
                side.append(
                    jnp.zeros((WM, LANES), F32)
                    if start is None
                    else sides[c, start : start + WM, :]
                )
            side.append(jnp.zeros((16 - nb * WM, LANES), F32))
            blocks[g, main + nb * 64 :, :] = jnp.concatenate(side, 0).astype(BF16)
    for out, k in zip(outs, parcels(refl)):
        out[...] = blocks[((me ^ k) + 2) % refl]


def far_places(refl):
    return list(range(4, refl, 2))


def parcels(refl):
    far = far_places(refl)
    return [k ^ 1 for k in far] + far + [0, 1, 2, 3]


def block_terms(spectra, rows):
    refl = rows * COLS
    freqs, receivers, width = spectra.shape[1:]
    nb = len(band_rows(0, rows))
    size = 2 * HF * WC + nb * 64 + 48
    return pl.pallas_call(
        functools.partial(terms_kernel, rows),
        in_specs=[pl.BlockSpec(memory_space=pl.ANY)],
        out_shape=[jax.ShapeDtypeStruct((size, LANES), BF16)] * refl,
        scratch_shapes=[
            pltpu.VMEM((freqs, 2, receivers, width), BF16),
            pltpu.VMEM((refl, size, LANES), BF16),
            pltpu.VMEM((refl, nb * 64, LANES), F32),
            pltpu.VMEM((COLS, rows * WC, LANES), F32),
            pltpu.SemaphoreType.DMA((freqs, 2)),
        ],
        compiler_params=pltpu.CompilerParams(vmem_limit_bytes=TERMS_VMEM),
        name="block_terms",
    )(spectra)


def project_kernel(r_ref, t_ref, keep_ref, send_ref):
    j = lax.axis_index("freq")
    table = jnp.concatenate([t_ref[j, TIME], t_ref[1 - j, TIME]], 0).astype(BF16)
    half = WC // 2
    for s in range(half):
        pair = jnp.concatenate([r_ref[s], r_ref[half + s]], 0)
        got = lax.dot_general(table, pair, (((1,), (1,)), ((), ())), preferred_element_type=F32)
        keep_ref[s] = got[: 2 * HF]
        send_ref[s] = got[2 * HF :]


def project(recorded, table):
    shape = jax.ShapeDtypeStruct((WC // 2, 2 * HF, LANES), F32)
    return pl.pallas_call(
        project_kernel, out_shape=[shape, shape], compiler_params=VMEM, name="project"
    )(recorded, table)


def grid_place(rows):
    g = (lax.axis_index("refl") + 2) % (rows * COLS)
    return g // COLS, g % COLS


def edge_kernel(rows, keep_ref, other_ref, *outs):
    bands, sides_ref = outs[:-1], outs[-1]
    j = lax.axis_index("freq")
    p, _ = grid_place(rows)
    half = WC // 2
    low = lanes_of(HF) < LANES // 2

    def build(out_ref, first, upper):
        for s in range(WM):
            for part in range(2):
                rows_of = pl.ds(part * HF, HF)
                kept = keep_ref[first + s, rows_of, :]
                other = other_ref[first + s, rows_of, :]
                a = jnp.where(j == 0, kept, other)
                b = jnp.where(j == 0, other, kept)
                plain = jnp.where(low, a, pltpu.roll(b, LANES // 2, 1))
                shifted = jnp.where(low, pltpu.roll(a, LANES // 2, 1), b)
                band = jnp.where(upper, shifted, plain)
                out_ref[pl.ds(part * WM + s, HF, stride=8), :] = band

    if rows == 2:
        build(bands[0], jnp.where(p == 0, half - WM, 0), p == 0)
    else:
        build(bands[0], half - WM, True)
        build(bands[1], 0, False)

    keep = keep_ref[...].reshape(half * 2 * HF, LANES)
    other = other_ref[...].reshape(half * 2 * HF, LANES)
    left = jnp.where(j == 0, keep, other).astype(BF16)
    right = jnp.where(j == 0, other, keep).astype(BF16)
    row = lax.broadcasted_iota(jnp.int32, (LANES, LANES), 0)
    r = lax.broadcasted_iota(jnp.int32, (LANES, LANES), 1) % 8
    at = lax.broadcasted_iota(jnp.int32, (half, 2 * HF, LANES), 1)
    lane = lax.broadcasted_iota(jnp.int32, (half, 2 * HF, LANES), 2)
    mine = (lane // 16 == at % HF) & ((lane // 8) % 2 == at // HF)
    for upper in range(2):
        from_right = ((row == upper * 64 + 60 + r) & (r < WM)).astype(F32).astype(BF16)
        from_left = ((row == upper * 64 + r - WM) & (r >= WM)).astype(F32).astype(BF16)
        x = jnp.dot(left, from_left, preferred_element_type=F32)
        x = x + jnp.dot(right, from_right, preferred_element_type=F32)
        x = jnp.where(mine, x.reshape(half, 2 * HF, LANES), 0.0)
        sides_ref[upper * half : (upper + 1) * half, :] = jnp.sum(x, 1)


def edge_projections(keep, other, rows):
    nb = len(band_rows(0, rows))
    return pl.pallas_call(
        functools.partial(edge_kernel, rows),
        out_shape=[jax.ShapeDtypeStruct((64, LANES), F32)] * nb
        + [jax.ShapeDtypeStruct((WC, LANES), F32)],
        compiler_params=VMEM,
        name="edge_projections",
    )(keep, other)


def statistics_kernel(rows, *refs):
    nb = len(band_rows(0, rows))
    count = rows * COLS // 2 + 2
    blocks, refs = refs[:count], refs[count:]
    keep_ref, other_ref, lags_ref = refs[:3]
    rims = [x[...] for x in refs[3 : 3 + nb * 3 + 2]]
    bands, nears, fars = rims[:nb], rims[nb : 2 * nb + 1], rims[2 * nb + 1 :]
    refs = refs[3 + nb * 3 + 2 :]
    bands = [x.astype(F32) for x in bands]
    own_ref, send_ref, lag_ref, spectrum = refs
    j = lax.axis_index("freq")
    p, c = grid_place(rows)
    half = WC // 2

    def summed(start, size):
        total = blocks[0][start : start + size, :].astype(F32)
        for block in blocks[1:]:
            total = total + block[start : start + size, :].astype(F32)
        return total.astype(BF16).astype(F32)

    low = lanes_of(half) < LANES // 2
    for fp in range(2 * HF):
        x = summed(fp * WC, WC)
        a, b = x[:half], x[half:]
        first = jnp.where(low, a, pltpu.roll(b, LANES // 2, 1))
        second = jnp.where(low, pltpu.roll(a, LANES // 2, 1), b)
        spectrum[pl.ds(fp, half, stride=16), :] = first
        spectrum[pl.ds(half * 16 + fp, half, stride=16), :] = second
    count = half * 16
    here = pl.multiple_of(j * count, count)
    there = pl.multiple_of((1 - j) * count, count)
    own_ref[...] = spectrum[pl.ds(here, count), :].astype(BF16)
    send_ref[...] = spectrum[pl.ds(there, count), :].astype(BF16)
    sums = []
    for at, q_ref in ((here, keep_ref), (there, other_ref)):
        power = in_phase = turned = jnp.zeros((HF, LANES), F32)
        for s in range(half):
            a = spectrum[pl.ds(at + s * 16, HF), :]
            b = spectrum[pl.ds(at + s * 16 + HF, HF), :]
            qc, qs = q_ref[s, :HF, :], q_ref[s, HF:, :]
            power = power + (a * a + b * b)
            in_phase = in_phase + (a * qc + b * qs)
            turned = turned + (b * qc - a * qs)
        sums.append([power, in_phase, turned])
    total = None
    sub = lax.broadcasted_iota(jnp.int32, (HF, 8, LANES), 1)
    for n in range(nb):
        x = summed(2 * HF * WC + n * 64, 64).reshape(HF, 8, LANES)
        q = bands[n].reshape(HF, 8, LANES)
        partner = jnp.where(sub < WM, -1.0, 1.0) * pltpu.roll(q, WM, 1)
        here_sums = [jnp.sum(x * y, 1) for y in (x, q, partner)]
        total = here_sums if total is None else [a + b for a, b in zip(total, here_sums)]
    sums.append(total)

    window = lax.broadcasted_iota(jnp.int32, (8, LANES), 0)
    lane = lanes_of(8)
    window = jnp.where(window < 4, (window + 2 * j) % 4, 8)
    starts = window * WC - WM

    def mask(receiver):
        return ((receiver >= starts) & (receiver < starts + WC + 2 * WM)).astype(F32)

    dot = functools.partial(lax.dot_general, precision=EXACT, preferred_element_type=F32)
    stats = jnp.zeros((8, 32), F32)
    receivers = (j * 64 + lane % 64, (1 - j) * 64 + lane % 64, lane)
    for x, receiver in zip(sums, receivers):
        x = jnp.concatenate(x + [jnp.zeros((HF, LANES), F32)], 0)
        stats = stats + dot(mask(receiver), x, (((1,), (1,)), ((), ())))
    x = summed(2 * HF * WC + nb * 64, 48)
    l48 = lanes_of(48)
    from_near = ((l48 % 8) < WM) == ((c % 2) == 1)
    q = []
    for sides in (nears, fars):
        sides = [x.astype(F32) for x in sides]
        pieces = [sides[0]]
        for n, side in enumerate(sides[1:]):
            top, bottom = side[:WM, :], side[WC - WM :, :]
            pieces.append(jnp.where(p == 0, top, bottom) if nb == 1 else (bottom, top)[n])
        pieces.append(jnp.zeros((16 - nb * WM, LANES), F32))
        q.append(jnp.concatenate(pieces, 0))
    q = jnp.where(from_near, q[0], q[1])
    first_part = (l48 // 8) % 2 == 0
    partner = jnp.where(first_part, -pltpu.roll(q, LANES - 8, 1), pltpu.roll(q, 8, 1))
    row = lax.broadcasted_iota(jnp.int32, (LANES, 32), 0)
    column = lax.broadcasted_iota(jnp.int32, (LANES, 32), 1)
    at_side = ((window == 0) & (lane % 8 < WM)) | ((window == 3) & (lane % 8 >= WM))
    for n, y in enumerate((x, q, partner)):
        z = jnp.sum(x * y, 0, keepdims=True)
        z = jnp.where(at_side, jnp.broadcast_to(z, (8, LANES)), 0.0)
        to = (column == n * HF + row // 16).astype(F32)
        stats = stats + dot(z, to, (((1,), (0,)), ((), ())))
    lag_ref[...] = dot(stats, lags_ref[j, LAGS], (((1,), (0,)), ((), ())))


def statistics(blocks, keep, other, table, bands, nears, fars, rows):
    count = WC // 2 * 2 * HF
    return pl.pallas_call(
        functools.partial(statistics_kernel, rows),
        out_shape=[
            jax.ShapeDtypeStruct((count, LANES), BF16),
            jax.ShapeDtypeStruct((count, LANES), BF16),
            jax.ShapeDtypeStruct((8, 2 * LANES), F32),
        ],
        scratch_shapes=[pltpu.VMEM((2 * count, LANES), F32)],
        compiler_params=VMEM,
        name="statistics",
    )(*blocks, keep, other, table, *bands, *nears, *fars)


def subtract_kernel(
    steps,
    lag_ref,
    lag_got_ref,
    start_ref,
    table_ref,
    own_ref,
    got_ref,
    r_low_ref,
    r_high_ref,
    clean_ref,
    filters_ref,
    wavelets,
):
    step = pl.program_id(0)
    j = lax.axis_index("freq")
    half = WC // 2

    @pl.when(step == 0)
    def _():
        total = lag_ref[0:2, :] + lag_got_ref[2:4, :]
        lag, target = total[:, :LANES], total[:, LANES:]
        lane = lanes_of(2)
        held = lane < TAPS
        magnitude = jnp.where(held, jnp.abs(lag), 0.0)
        zero_lag = jnp.sum(jnp.where(lane == 0, lag, 0.0), 1, keepdims=True)
        others = jnp.sum(jnp.where(lane >= 1, magnitude, 0.0), 1, keepdims=True)
        step_size = 0.5 / (zero_lag + 2.0 * others + 1e-06)
        filters = jnp.concatenate(
            [start_ref[...], jnp.zeros((2, LANES - TAPS), F32)], 1
        )
        spread = [jnp.broadcast_to(lag[:, d : d + 1], (2, LANES)) for d in range(TAPS)]
        for repeat in range(ITERS):
            applied = spread[0] * filters
            for d in range(1, TAPS):
                applied = applied + spread[d] * (
                    pltpu.roll(filters, d, 1) + pltpu.roll(filters, LANES - d, 1)
                )
            filters = jnp.where(held, filters + step_size * (target - applied), 0.0)
        filters_ref[...] = filters[:, :TAPS]
        taps = filters.astype(BF16).astype(F32)
        for w in range(2):
            for n, h in enumerate((j, 1 - j)):
                tap = taps[w : w + 1, :]
                hc = jnp.sum(table_ref[h, TRIG, :LANES] * tap, 1, keepdims=True)
                hs = jnp.sum(table_ref[h, TRIG, LANES:] * tap, 1, keepdims=True)
                wave = hc * table_ref[h, TIME] + hs * table_ref[h, TURNED]
                at = w * 32 + n * 16
                wavelets[at : at + 16, :] = wave.astype(BF16)

    table = wavelets[...]
    lane = lax.broadcasted_iota(jnp.int32, (32, LANES), 1)
    first = (lane % 64) < WC
    zero = jnp.zeros((32, LANES), BF16)
    for s in range(half // steps):
        x = jnp.concatenate([own_ref[s * 16 : s * 16 + 16, :], got_ref[s * 16 : s * 16 + 16, :]], 0)
        both = jnp.concatenate([jnp.where(first, x, zero), jnp.where(first, zero, x)], 0)
        predicted = lax.dot_general(
            both, table, (((0,), (0,)), ((), ())), preferred_element_type=F32
        )
        clean_ref[0, s] = (r_low_ref[0, s].astype(F32) - predicted[:64]).astype(BF16)
        clean_ref[1, s] = (r_high_ref[0, s].astype(F32) - predicted[64:]).astype(BF16)


def subtract(lag, lag_got, start, table, own, got, recorded):
    steps = 2
    half = WC // 2
    each = half // steps
    recorded = recorded.reshape(2, half, 64, NT)
    whole = lambda x: pl.BlockSpec(x.shape, lambda i: (0,) * x.ndim)
    small = (lag, lag_got, start, table)
    rows_spec = pl.BlockSpec((each * 16, LANES), lambda i: (i, 0))
    return pl.pallas_call(
        functools.partial(subtract_kernel, steps),
        grid=(steps,),
        in_specs=[whole(x) for x in small]
        + [
            rows_spec,
            rows_spec,
            pl.BlockSpec((1, each, 64, NT), lambda i: (0, i, 0, 0)),
            pl.BlockSpec((1, each, 64, NT), lambda i: (1, i, 0, 0)),
        ],
        out_specs=[
            pl.BlockSpec((2, each, 64, NT), lambda i: (0, i, 0, 0)),
            pl.BlockSpec((2, TAPS), lambda i: (0, 0)),
        ],
        out_shape=[
            jax.ShapeDtypeStruct((2, half, 64, NT), BF16),
            jax.ShapeDtypeStruct((2, TAPS), F32),
        ],
        scratch_shapes=[pltpu.VMEM((64, NT), BF16)],
        compiler_params=VMEM,
        name="subtract",
    )(*small, own, got, recorded, recorded)


def body(spectra, recorded, initial_filters):
    refl = lax.axis_size("refl")
    rows = refl // COLS
    table = jnp.asarray(tables())
    core_swap = [(0, 1), (1, 0)]

    def place(p, c):
        return (p * COLS + c - 2) % refl

    def swap(x, k):
        return lax.ppermute(x, "refl", [(i, i ^ k) for i in range(refl)])

    def add(x, y):
        return (x.astype(F32) + y.astype(F32)).astype(BF16)

    after = lax.optimization_barrier
    blocks = block_terms(spectra, rows)
    far = far_places(refl)
    sent, kept, close = list(blocks[: len(far)]), blocks[len(far) : -4], blocks[-4:]
    came = [swap(sent[0], 1)]
    tile, sent[1] = after((recorded[0, 0], sent[1]))
    keep, send = project(tile, table)
    other = lax.ppermute(send, "freq", core_swap)
    *bands, sides = edge_projections(keep, other, rows)
    extra = {}
    if rows == 2:
        near = swap(sides, 1)
        extra = {6: [near], 4: [bands[0], near], 2: [near]}

    def parcel(block, k):
        return jnp.concatenate([block] + [x.astype(BF16) for x in extra.get(k, [])])

    totals = [parcel(add(kept[0], came[0]), far[0])]
    totals[0], *sent[1:] = after((totals[0], *sent[1:]))
    came += [swap(x, 1) for x in sent[1:]]
    totals += [parcel(add(kept[n], came[n]), far[n]) for n in range(1, len(far))]
    got = [swap(x, k) for x, k in zip(totals, far)]
    own, *close = close
    (close[0], close[2]), _ = after(((close[0], close[2]), totals[1]))
    close[1], _ = after((close[1], totals[0]))
    close = [swap(parcel(x, k), k) for k, x in enumerate(close, 1)]
    size = own.shape[0]
    if rows == 2:
        bands = [got[0][size : size + 64]]
        nears, fars = [near, got[0][size + 64 :]], [got[1][size:], close[1][size:]]
    else:

        def shift(x, rise, across):
            route = [
                (place(p, c), place(p + rise, across[c]))
                for p in range(rows)
                for c in range(COLS)
                if 0 <= p + rise < rows and across[c] is not None
            ]
            return lax.ppermute(x, "refl", route)

        bands = [shift(x, rise, (0, 1, 2, 3)) for x, rise in zip(bands, (1, -1))]
        nears = [shift(sides, rise, (1, 0, 3, 2)) for rise in (0, 1, -1)]
        fars = [shift(sides, rise, (None, 2, 1, None)) for rise in (0, 1, -1)]
    own, away, lag = statistics([own] + got + close, keep, other, table, bands, nears, fars, rows)
    away_got = lax.ppermute(away, "freq", core_swap)
    lag_got = lax.ppermute(lag, "freq", core_swap)
    clean, filters = subtract(
        lag,
        lag_got,
        initial_filters.reshape(2, TAPS),
        table,
        own,
        away_got,
        tile,
    )
    return (clean.reshape(recorded.shape), filters.reshape(initial_filters.shape))


def solution(mesh):
    placed = (
        P(None, "freq", "groups", "refl"),
        P("refl", "freq", "groups", None, None),
        P("refl", "freq", "groups", None, None),
    )
    return jax.shard_map(
        body,
        mesh=mesh,
        in_specs=placed,
        out_specs=(
            P("refl", "freq", "groups", None, None),
            P("refl", "freq", "groups", None, None),
        ),
        check_vma=False,
    )
```

```python
import functools
import math

import jax
import jax.numpy as jnp
import numpy as np
from jax import lax
from jax.experimental import pallas as pl
from jax.experimental.pallas import tpu as pltpu
from jax.sharding import PartitionSpec as P

NF = 16
K0 = 48
NT = 256
XR = 8192
WC = 32
WM = 4
TAPS = 33
ITERS = 3
HALF = (TAPS - 1) // 2
COLS = 4
LANES = 128
HF = 8
TERMS_VMEM = 48 * 1024 * 1024
AHEAD = 3
EXACT = lax.Precision.HIGHEST
F32 = jnp.float32
BF16 = jnp.bfloat16
VMEM = pltpu.CompilerParams(vmem_limit_bytes=12 * 1024 * 1024)


def tables():
    f = np.arange(NF)
    t = np.arange(NT)
    w = 2.0 * np.pi * (K0 + f) / NT
    angle = 2.0 * np.pi * (((K0 + f)[:, None] * t[None, :]) % NT) / NT
    weight = math.sqrt(2.0 / NF)
    table = np.stack([weight * np.cos(angle), -weight * np.sin(angle)], 1)
    table = table.astype(np.float32).astype(jnp.bfloat16).astype(np.float32)
    halves = table.reshape(2, HF, 2, NT).transpose(0, 2, 1, 3)
    time = halves.reshape(2, 2 * HF, NT)
    turned = np.stack([-halves[:, 1], halves[:, 0]], 1).reshape(2, 2 * HF, NT)
    lane = np.arange(LANES)
    held = lane < TAPS
    tap = lane - HALF
    cos_k = np.where(held, np.cos(w[:, None] * tap), 0.0).reshape(2, HF, LANES)
    sin_k = np.where(held, np.sin(w[:, None] * tap), 0.0).reshape(2, HF, LANES)
    lag = np.where(held, 16.0 * np.cos(w[:, None] * lane), 0.0).reshape(2, HF, LANES)
    zero = np.zeros_like(lag)
    to_lag = np.concatenate([lag, zero, zero, zero], 1)
    to_target = np.concatenate([zero, cos_k, sin_k, zero], 1)
    lags = np.concatenate([to_lag, to_target], 2)
    trig = np.concatenate([np.concatenate([cos_k, cos_k], 1), np.concatenate([sin_k, sin_k], 1)], 2)
    return np.concatenate([time, turned, lags, trig], 1).astype(np.float32)


TIME, TURNED, LAGS, TRIG = (slice(0, 16), slice(16, 32), slice(32, 64), slice(64, 80))


def lanes_of(rows):
    return lax.broadcasted_iota(jnp.int32, (rows, LANES), 1)


def band_rows(p, rows):
    if rows == 2:
        return [WC if p == 0 else WC - WM]
    return [p * WC - WM if p > 0 else None, (p + 1) * WC if p < rows - 1 else None]


def terms_kernel(rows, s_hbm, *rest):
    refl = rows * COLS
    outs, (buffer, blocks, bands, sides, arrived) = rest[:-5], rest[-5:]
    sources = rows * WC
    freqs, _, _, width = buffer.shape
    amplitude = 1.0 / math.sqrt(2.0 * XR)
    nb = len(band_rows(0, rows))
    main = 2 * HF * WC

    def fetch(f, part):
        return pltpu.make_async_copy(s_hbm.at[part, f], buffer.at[f, part], arrived.at[f, part])

    for f in range(AHEAD):
        for part in range(2):
            fetch(f, part).start()

    def products(f):
        if f + AHEAD < freqs:
            for part in range(2):
                fetch(f + AHEAD, part).start()
        for part in range(2):
            fetch(f, part).wait()
        left = buffer[f, :, :sources, :].reshape(2 * sources, width)
        parts = [[], []]
        for c in range(COLS):
            right = buffer[f, :, c * LANES : (c + 1) * LANES, :].reshape(2 * LANES, width)
            got = lax.dot_general(left, right, (((1,), (1,)), ((), ())), preferred_element_type=F32)
            parts[0].append(amplitude * (got[:sources, :LANES] - got[sources:, LANES:]))
            parts[1].append(amplitude * (got[:sources, LANES:] + got[sources:, :LANES]))
        return parts

    def place(f, parts):
        for c in range(COLS):
            for p in range(rows):
                g = p * COLS + c
                for part in range(2):
                    at = part * HF * WC + f * WC
                    x = parts[part][c][p * WC : (p + 1) * WC]
                    blocks[g, at : at + WC, :] = x.astype(BF16)
                for n, start in enumerate(band_rows(p, rows)):
                    if start is None:
                        band = jnp.zeros((2 * WM, LANES), F32)
                    else:
                        band = jnp.concatenate([x[c][start : start + WM] for x in parts], 0)
                    bands[g, n * HF * 8 + f * 8 : n * HF * 8 + f * 8 + 8, :] = band
        lane = lanes_of(sources)
        base = f * 16
        first = (lane >= base) & (lane < base + 8)
        second = (lane >= base + 8) & (lane < base + 16)
        zero = jnp.zeros((sources, LANES), F32)
        for c in range(COLS):
            side = sides[c]
            for part, here in enumerate((first, second)):
                x = parts[part]
                before = x[c - 1] if c > 0 else zero
                after = x[c + 1] if c < COLS - 1 else zero
                moved = jnp.where(lane >= LANES // 2, before, after)
                moved = pltpu.roll(moved, (base + part * 8 + WM) % LANES, 1)
                side = jnp.where(here, moved, side)
            sides[c] = side

    before = None
    for f in range(freqs):
        parts = products(f)
        if before is not None:
            place(f - 1, before)
        before = parts
    place(freqs - 1, before)
    me = lax.axis_index("refl")
    for p in range(rows):
        for c in range(COLS):
            g = p * COLS + c
            blocks[g, main : main + nb * 64, :] = bands[g].astype(BF16)
            side = [sides[c, p * WC : (p + 1) * WC, :]]
            for start in band_rows(p, rows):
                side.append(
                    jnp.zeros((WM, LANES), F32)
                    if start is None
                    else sides[c, start : start + WM, :]
                )
            side.append(jnp.zeros((16 - nb * WM, LANES), F32))
            blocks[g, main + nb * 64 :, :] = jnp.concatenate(side, 0).astype(BF16)
    for out, k in zip(outs, parcels(refl)):
        out[...] = blocks[((me ^ k) + 2) % refl]


def far_places(refl):
    return list(range(4, refl, 2))


def parcels(refl):
    far = far_places(refl)
    return [k ^ 1 for k in far] + far + [0, 1, 2, 3]


def block_terms(spectra, rows):
    refl = rows * COLS
    freqs, receivers, width = spectra.shape[1:]
    nb = len(band_rows(0, rows))
    size = 2 * HF * WC + nb * 64 + 48
    return pl.pallas_call(
        functools.partial(terms_kernel, rows),
        in_specs=[pl.BlockSpec(memory_space=pl.ANY)],
        out_shape=[jax.ShapeDtypeStruct((size, LANES), BF16)] * refl,
        scratch_shapes=[
            pltpu.VMEM((freqs, 2, receivers, width), BF16),
            pltpu.VMEM((refl, size, LANES), BF16),
            pltpu.VMEM((refl, nb * 64, LANES), F32),
            pltpu.VMEM((COLS, rows * WC, LANES), F32),
            pltpu.SemaphoreType.DMA((freqs, 2)),
        ],
        compiler_params=pltpu.CompilerParams(vmem_limit_bytes=TERMS_VMEM),
        name="block_terms",
    )(spectra)


def project_kernel(r_ref, t_ref, keep_ref, send_ref):
    j = lax.axis_index("freq")
    table = jnp.concatenate([t_ref[j, TIME], t_ref[1 - j, TIME]], 0).astype(BF16)
    half = WC // 2
    for s in range(half):
        pair = jnp.concatenate([r_ref[s], r_ref[half + s]], 0)
        got = lax.dot_general(table, pair, (((1,), (1,)), ((), ())), preferred_element_type=F32)
        keep_ref[s] = got[: 2 * HF]
        send_ref[s] = got[2 * HF :]


def project(recorded, table):
    shape = jax.ShapeDtypeStruct((WC // 2, 2 * HF, LANES), F32)
    return pl.pallas_call(
        project_kernel, out_shape=[shape, shape], compiler_params=VMEM, name="project"
    )(recorded, table)


def grid_place(rows):
    g = (lax.axis_index("refl") + 2) % (rows * COLS)
    return g // COLS, g % COLS


def edge_kernel(rows, keep_ref, other_ref, *outs):
    bands, sides_ref = outs[:-1], outs[-1]
    j = lax.axis_index("freq")
    p, _ = grid_place(rows)
    half = WC // 2
    low = lanes_of(HF) < LANES // 2

    def build(out_ref, first, upper):
        for s in range(WM):
            for part in range(2):
                rows_of = pl.ds(part * HF, HF)
                kept = keep_ref[first + s, rows_of, :]
                other = other_ref[first + s, rows_of, :]
                a = jnp.where(j == 0, kept, other)
                b = jnp.where(j == 0, other, kept)
                plain = jnp.where(low, a, pltpu.roll(b, LANES // 2, 1))
                shifted = jnp.where(low, pltpu.roll(a, LANES // 2, 1), b)
                band = jnp.where(upper, shifted, plain)
                out_ref[pl.ds(part * WM + s, HF, stride=8), :] = band

    if rows == 2:
        build(bands[0], jnp.where(p == 0, half - WM, 0), p == 0)
    else:
        build(bands[0], half - WM, True)
        build(bands[1], 0, False)

    keep = keep_ref[...].reshape(half * 2 * HF, LANES)
    other = other_ref[...].reshape(half * 2 * HF, LANES)
    left = jnp.where(j == 0, keep, other).astype(BF16)
    right = jnp.where(j == 0, other, keep).astype(BF16)
    row = lax.broadcasted_iota(jnp.int32, (LANES, LANES), 0)
    r = lax.broadcasted_iota(jnp.int32, (LANES, LANES), 1) % 8
    at = lax.broadcasted_iota(jnp.int32, (half, 2 * HF, LANES), 1)
    lane = lax.broadcasted_iota(jnp.int32, (half, 2 * HF, LANES), 2)
    mine = (lane // 16 == at % HF) & ((lane // 8) % 2 == at // HF)
    for upper in range(2):
        from_right = ((row == upper * 64 + 60 + r) & (r < WM)).astype(F32).astype(BF16)
        from_left = ((row == upper * 64 + r - WM) & (r >= WM)).astype(F32).astype(BF16)
        x = jnp.dot(left, from_left, preferred_element_type=F32)
        x = x + jnp.dot(right, from_right, preferred_element_type=F32)
        x = jnp.where(mine, x.reshape(half, 2 * HF, LANES), 0.0)
        sides_ref[upper * half : (upper + 1) * half, :] = jnp.sum(x, 1)


def edge_projections(keep, other, rows):
    nb = len(band_rows(0, rows))
    return pl.pallas_call(
        functools.partial(edge_kernel, rows),
        out_shape=[jax.ShapeDtypeStruct((64, LANES), F32)] * nb
        + [jax.ShapeDtypeStruct((WC, LANES), F32)],
        compiler_params=VMEM,
        name="edge_projections",
    )(keep, other)


def statistics_kernel(rows, *refs):
    nb = len(band_rows(0, rows))
    count = rows * COLS // 2 + 2
    blocks, refs = refs[:count], refs[count:]
    keep_ref, other_ref, lags_ref = refs[:3]
    rims = [x[...] for x in refs[3 : 3 + nb * 3 + 2]]
    bands, nears, fars = rims[:nb], rims[nb : 2 * nb + 1], rims[2 * nb + 1 :]
    refs = refs[3 + nb * 3 + 2 :]
    bands = [x.astype(F32) for x in bands]
    own_ref, send_ref, lag_ref, spectrum = refs
    j = lax.axis_index("freq")
    p, c = grid_place(rows)
    half = WC // 2

    def summed(start, size):
        total = blocks[0][start : start + size, :].astype(F32)
        for block in blocks[1:]:
            total = total + block[start : start + size, :].astype(F32)
        return total.astype(BF16).astype(F32)

    low = lanes_of(half) < LANES // 2
    for fp in range(2 * HF):
        x = summed(fp * WC, WC)
        a, b = x[:half], x[half:]
        first = jnp.where(low, a, pltpu.roll(b, LANES // 2, 1))
        second = jnp.where(low, pltpu.roll(a, LANES // 2, 1), b)
        spectrum[pl.ds(fp, half, stride=16), :] = first
        spectrum[pl.ds(half * 16 + fp, half, stride=16), :] = second
    count = half * 16
    here = pl.multiple_of(j * count, count)
    there = pl.multiple_of((1 - j) * count, count)
    own_ref[...] = spectrum[pl.ds(here, count), :].astype(BF16)
    send_ref[...] = spectrum[pl.ds(there, count), :].astype(BF16)
    sums = []
    for at, q_ref in ((here, keep_ref), (there, other_ref)):
        power = in_phase = turned = jnp.zeros((HF, LANES), F32)
        for s in range(half):
            a = spectrum[pl.ds(at + s * 16, HF), :]
            b = spectrum[pl.ds(at + s * 16 + HF, HF), :]
            qc, qs = q_ref[s, :HF, :], q_ref[s, HF:, :]
            power = power + (a * a + b * b)
            in_phase = in_phase + (a * qc + b * qs)
            turned = turned + (b * qc - a * qs)
        sums.append([power, in_phase, turned])
    total = None
    sub = lax.broadcasted_iota(jnp.int32, (HF, 8, LANES), 1)
    for n in range(nb):
        x = summed(2 * HF * WC + n * 64, 64).reshape(HF, 8, LANES)
        q = bands[n].reshape(HF, 8, LANES)
        partner = jnp.where(sub < WM, -1.0, 1.0) * pltpu.roll(q, WM, 1)
        here_sums = [jnp.sum(x * y, 1) for y in (x, q, partner)]
        total = here_sums if total is None else [a + b for a, b in zip(total, here_sums)]
    sums.append(total)

    window = lax.broadcasted_iota(jnp.int32, (8, LANES), 0)
    lane = lanes_of(8)
    window = jnp.where(window < 4, (window + 2 * j) % 4, 8)
    starts = window * WC - WM

    def mask(receiver):
        return ((receiver >= starts) & (receiver < starts + WC + 2 * WM)).astype(F32)

    dot = functools.partial(lax.dot_general, precision=EXACT, preferred_element_type=F32)
    stats = jnp.zeros((8, 32), F32)
    receivers = (j * 64 + lane % 64, (1 - j) * 64 + lane % 64, lane)
    for x, receiver in zip(sums, receivers):
        x = jnp.concatenate(x + [jnp.zeros((HF, LANES), F32)], 0)
        stats = stats + dot(mask(receiver), x, (((1,), (1,)), ((), ())))
    x = summed(2 * HF * WC + nb * 64, 48)
    l48 = lanes_of(48)
    from_near = ((l48 % 8) < WM) == ((c % 2) == 1)
    q = []
    for sides in (nears, fars):
        sides = [x.astype(F32) for x in sides]
        pieces = [sides[0]]
        for n, side in enumerate(sides[1:]):
            top, bottom = side[:WM, :], side[WC - WM :, :]
            pieces.append(jnp.where(p == 0, top, bottom) if nb == 1 else (bottom, top)[n])
        pieces.append(jnp.zeros((16 - nb * WM, LANES), F32))
        q.append(jnp.concatenate(pieces, 0))
    q = jnp.where(from_near, q[0], q[1])
    first_part = (l48 // 8) % 2 == 0
    partner = jnp.where(first_part, -pltpu.roll(q, LANES - 8, 1), pltpu.roll(q, 8, 1))
    row = lax.broadcasted_iota(jnp.int32, (LANES, 32), 0)
    column = lax.broadcasted_iota(jnp.int32, (LANES, 32), 1)
    at_side = ((window == 0) & (lane % 8 < WM)) | ((window == 3) & (lane % 8 >= WM))
    for n, y in enumerate((x, q, partner)):
        z = jnp.sum(x * y, 0, keepdims=True)
        z = jnp.where(at_side, jnp.broadcast_to(z, (8, LANES)), 0.0)
        to = (column == n * HF + row // 16).astype(F32)
        stats = stats + dot(z, to, (((1,), (0,)), ((), ())))
    lag_ref[...] = dot(stats, lags_ref[j, LAGS], (((1,), (0,)), ((), ())))


def statistics(blocks, keep, other, table, bands, nears, fars, rows):
    count = WC // 2 * 2 * HF
    return pl.pallas_call(
        functools.partial(statistics_kernel, rows),
        out_shape=[
            jax.ShapeDtypeStruct((count, LANES), BF16),
            jax.ShapeDtypeStruct((count, LANES), BF16),
            jax.ShapeDtypeStruct((8, 2 * LANES), F32),
        ],
        scratch_shapes=[pltpu.VMEM((2 * count, LANES), F32)],
        compiler_params=VMEM,
        name="statistics",
    )(*blocks, keep, other, table, *bands, *nears, *fars)


def subtract_kernel(
    steps,
    lag_ref,
    lag_got_ref,
    start_ref,
    table_ref,
    own_ref,
    got_ref,
    r_low_ref,
    r_high_ref,
    clean_ref,
    filters_ref,
    wavelets,
):
    step = pl.program_id(0)
    j = lax.axis_index("freq")
    half = WC // 2

    @pl.when(step == 0)
    def _():
        total = lag_ref[0:2, :] + lag_got_ref[2:4, :]
        lag, target = total[:, :LANES], total[:, LANES:]
        lane = lanes_of(2)
        held = lane < TAPS
        magnitude = jnp.where(held, jnp.abs(lag), 0.0)
        zero_lag = jnp.sum(jnp.where(lane == 0, lag, 0.0), 1, keepdims=True)
        others = jnp.sum(jnp.where(lane >= 1, magnitude, 0.0), 1, keepdims=True)
        step_size = 0.5 / (zero_lag + 2.0 * others + 1e-06)
        filters = jnp.concatenate(
            [start_ref[...], jnp.zeros((2, LANES - TAPS), F32)], 1
        )
        spread = [jnp.broadcast_to(lag[:, d : d + 1], (2, LANES)) for d in range(TAPS)]
        for repeat in range(ITERS):
            applied = spread[0] * filters
            for d in range(1, TAPS):
                applied = applied + spread[d] * (
                    pltpu.roll(filters, d, 1) + pltpu.roll(filters, LANES - d, 1)
                )
            filters = jnp.where(held, filters + step_size * (target - applied), 0.0)
        filters_ref[...] = filters[:, :TAPS]
        taps = filters.astype(BF16).astype(F32)
        for w in range(2):
            for n, h in enumerate((j, 1 - j)):
                tap = taps[w : w + 1, :]
                hc = jnp.sum(table_ref[h, TRIG, :LANES] * tap, 1, keepdims=True)
                hs = jnp.sum(table_ref[h, TRIG, LANES:] * tap, 1, keepdims=True)
                wave = hc * table_ref[h, TIME] + hs * table_ref[h, TURNED]
                at = w * 32 + n * 16
                wavelets[at : at + 16, :] = wave.astype(BF16)

    table = wavelets[...]
    lane = lax.broadcasted_iota(jnp.int32, (32, LANES), 1)
    first = (lane % 64) < WC
    zero = jnp.zeros((32, LANES), BF16)
    for s in range(half // steps):
        x = jnp.concatenate([own_ref[s * 16 : s * 16 + 16, :], got_ref[s * 16 : s * 16 + 16, :]], 0)
        both = jnp.concatenate([jnp.where(first, x, zero), jnp.where(first, zero, x)], 0)
        predicted = lax.dot_general(
            both, table, (((0,), (0,)), ((), ())), preferred_element_type=F32
        )
        clean_ref[0, s] = (r_low_ref[0, s].astype(F32) - predicted[:64]).astype(BF16)
        clean_ref[1, s] = (r_high_ref[0, s].astype(F32) - predicted[64:]).astype(BF16)


def subtract(lag, lag_got, start, table, own, got, recorded):
    steps = 2
    half = WC // 2
    each = half // steps
    recorded = recorded.reshape(2, half, 64, NT)
    whole = lambda x: pl.BlockSpec(x.shape, lambda i: (0,) * x.ndim)
    small = (lag, lag_got, start, table)
    rows_spec = pl.BlockSpec((each * 16, LANES), lambda i: (i, 0))
    return pl.pallas_call(
        functools.partial(subtract_kernel, steps),
        grid=(steps,),
        in_specs=[whole(x) for x in small]
        + [
            rows_spec,
            rows_spec,
            pl.BlockSpec((1, each, 64, NT), lambda i: (0, i, 0, 0)),
            pl.BlockSpec((1, each, 64, NT), lambda i: (1, i, 0, 0)),
        ],
        out_specs=[
            pl.BlockSpec((2, each, 64, NT), lambda i: (0, i, 0, 0)),
            pl.BlockSpec((2, TAPS), lambda i: (0, 0)),
        ],
        out_shape=[
            jax.ShapeDtypeStruct((2, half, 64, NT), BF16),
            jax.ShapeDtypeStruct((2, TAPS), F32),
        ],
        scratch_shapes=[pltpu.VMEM((64, NT), BF16)],
        compiler_params=VMEM,
        name="subtract",
    )(*small, own, got, recorded, recorded)


def body(spectra, recorded, initial_filters):
    refl = lax.axis_size("refl")
    rows = refl // COLS
    table = jnp.asarray(tables())
    core_swap = [(0, 1), (1, 0)]

    def place(p, c):
        return (p * COLS + c - 2) % refl

    def swap(x, k):
        return lax.ppermute(x, "refl", [(i, i ^ k) for i in range(refl)])

    def add(x, y):
        return (x.astype(F32) + y.astype(F32)).astype(BF16)

    after = lax.optimization_barrier
    blocks = block_terms(spectra, rows)
    far = far_places(refl)
    sent, kept, close = list(blocks[: len(far)]), blocks[len(far) : -4], blocks[-4:]
    came = [swap(sent[0], 1)]
    tile, sent[1] = after((recorded[0, 0], sent[1]))
    keep, send = project(tile, table)
    other = lax.ppermute(send, "freq", core_swap)
    *bands, sides = edge_projections(keep, other, rows)
    extra = {}
    if rows == 2:
        near = swap(sides, 1)
        extra = {6: [near], 4: [bands[0], near], 3: [sides]}

    def parcel(block, k):
        return jnp.concatenate([block] + [x.astype(BF16) for x in extra.get(k, [])])

    totals = [parcel(add(kept[0], came[0]), far[0])]
    totals[0], *sent[1:] = after((totals[0], *sent[1:]))
    came += [swap(x, 1) for x in sent[1:]]
    totals += [parcel(add(kept[n], came[n]), far[n]) for n in range(1, len(far))]
    got = [swap(x, k) for x, k in zip(totals, far)]
    own, *close = close
    (close[0], close[1]), _ = after(((close[0], close[1]), totals[1]))
    close[2], _ = after((close[2], totals[0]))
    close = [swap(parcel(x, k), k) for k, x in enumerate(close, 1)]
    size = own.shape[0]
    if rows == 2:
        bands = [got[0][size : size + 64]]
        nears, fars = [near, got[0][size + 64 :]], [got[1][size:], close[2][size:]]
    else:

        def shift(x, rise, across):
            route = [
                (place(p, c), place(p + rise, across[c]))
                for p in range(rows)
                for c in range(COLS)
                if 0 <= p + rise < rows and across[c] is not None
            ]
            return lax.ppermute(x, "refl", route)

        bands = [shift(x, rise, (0, 1, 2, 3)) for x, rise in zip(bands, (1, -1))]
        nears = [shift(sides, rise, (1, 0, 3, 2)) for rise in (0, 1, -1)]
        fars = [shift(sides, rise, (None, 2, 1, None)) for rise in (0, 1, -1)]
    own, away, lag = statistics([own] + got + close, keep, other, table, bands, nears, fars, rows)
    away_got = lax.ppermute(away, "freq", core_swap)
    lag_got = lax.ppermute(lag, "freq", core_swap)
    clean, filters = subtract(
        lag,
        lag_got,
        initial_filters.reshape(2, TAPS),
        table,
        own,
        away_got,
        tile,
    )
    return (clean.reshape(recorded.shape), filters.reshape(initial_filters.shape))


def solution(mesh):
    placed = (
        P(None, "freq", "groups", "refl"),
        P("refl", "freq", "groups", None, None),
        P("refl", "freq", "groups", None, None),
    )
    return jax.shard_map(
        body,
        mesh=mesh,
        in_specs=placed,
        out_specs=(
            P("refl", "freq", "groups", None, None),
            P("refl", "freq", "groups", None, None),
        ),
        check_vma=False,
    )
```

```python
import functools
import math

import jax
import jax.numpy as jnp
import numpy as np
from jax import lax
from jax.experimental import pallas as pl
from jax.experimental.pallas import tpu as pltpu
from jax.sharding import PartitionSpec as P

NF = 16
K0 = 48
NT = 256
XR = 8192
WC = 32
WM = 4
TAPS = 33
ITERS = 3
HALF = (TAPS - 1) // 2
COLS = 4
LANES = 128
HF = 8
TERMS_VMEM = 48 * 1024 * 1024
AHEAD = 3
EXACT = lax.Precision.HIGHEST
F32 = jnp.float32
BF16 = jnp.bfloat16
VMEM = pltpu.CompilerParams(vmem_limit_bytes=12 * 1024 * 1024)


def tables():
    f = np.arange(NF)
    t = np.arange(NT)
    w = 2.0 * np.pi * (K0 + f) / NT
    angle = 2.0 * np.pi * (((K0 + f)[:, None] * t[None, :]) % NT) / NT
    weight = math.sqrt(2.0 / NF)
    table = np.stack([weight * np.cos(angle), -weight * np.sin(angle)], 1)
    table = table.astype(np.float32).astype(jnp.bfloat16).astype(np.float32)
    halves = table.reshape(2, HF, 2, NT).transpose(0, 2, 1, 3)
    time = halves.reshape(2, 2 * HF, NT)
    turned = np.stack([-halves[:, 1], halves[:, 0]], 1).reshape(2, 2 * HF, NT)
    lane = np.arange(LANES)
    held = lane < TAPS
    tap = lane - HALF
    cos_k = np.where(held, np.cos(w[:, None] * tap), 0.0).reshape(2, HF, LANES)
    sin_k = np.where(held, np.sin(w[:, None] * tap), 0.0).reshape(2, HF, LANES)
    lag = np.where(held, 16.0 * np.cos(w[:, None] * lane), 0.0).reshape(2, HF, LANES)
    zero = np.zeros_like(lag)
    to_lag = np.concatenate([lag, zero, zero, zero], 1)
    to_target = np.concatenate([zero, cos_k, sin_k, zero], 1)
    lags = np.concatenate([to_lag, to_target], 2)
    trig = np.concatenate([np.concatenate([cos_k, cos_k], 1), np.concatenate([sin_k, sin_k], 1)], 2)
    return np.concatenate([time, turned, lags, trig], 1).astype(np.float32)


TIME, TURNED, LAGS, TRIG = (slice(0, 16), slice(16, 32), slice(32, 64), slice(64, 80))


def lanes_of(rows):
    return lax.broadcasted_iota(jnp.int32, (rows, LANES), 1)


def band_rows(p, rows):
    if rows == 2:
        return [WC if p == 0 else WC - WM]
    return [p * WC - WM if p > 0 else None, (p + 1) * WC if p < rows - 1 else None]


def terms_kernel(rows, s_hbm, *rest):
    refl = rows * COLS
    outs, (buffer, blocks, bands, sides, arrived) = rest[:-5], rest[-5:]
    sources = rows * WC
    freqs, _, _, width = buffer.shape
    amplitude = 1.0 / math.sqrt(2.0 * XR)
    nb = len(band_rows(0, rows))
    main = 2 * HF * WC

    def fetch(f, part):
        return pltpu.make_async_copy(s_hbm.at[part, f], buffer.at[f, part], arrived.at[f, part])

    for f in range(AHEAD):
        for part in range(2):
            fetch(f, part).start()

    def products(f):
        if f + AHEAD < freqs:
            for part in range(2):
                fetch(f + AHEAD, part).start()
        for part in range(2):
            fetch(f, part).wait()
        left = buffer[f, :, :sources, :].reshape(2 * sources, width)
        parts = [[], []]
        for c in range(COLS):
            right = buffer[f, :, c * LANES : (c + 1) * LANES, :].reshape(2 * LANES, width)
            got = lax.dot_general(left, right, (((1,), (1,)), ((), ())), preferred_element_type=F32)
            parts[0].append(amplitude * (got[:sources, :LANES] - got[sources:, LANES:]))
            parts[1].append(amplitude * (got[:sources, LANES:] + got[sources:, :LANES]))
        return parts

    def place(f, parts):
        for c in range(COLS):
            for p in range(rows):
                g = p * COLS + c
                for part in range(2):
                    at = part * HF * WC + f * WC
                    x = parts[part][c][p * WC : (p + 1) * WC]
                    blocks[g, at : at + WC, :] = x.astype(BF16)
                for n, start in enumerate(band_rows(p, rows)):
                    if start is None:
                        band = jnp.zeros((2 * WM, LANES), F32)
                    else:
                        band = jnp.concatenate([x[c][start : start + WM] for x in parts], 0)
                    bands[g, n * HF * 8 + f * 8 : n * HF * 8 + f * 8 + 8, :] = band
        lane = lanes_of(sources)
        base = f * 16
        first = (lane >= base) & (lane < base + 8)
        second = (lane >= base + 8) & (lane < base + 16)
        zero = jnp.zeros((sources, LANES), F32)
        for c in range(COLS):
            side = sides[c]
            for part, here in enumerate((first, second)):
                x = parts[part]
                before = x[c - 1] if c > 0 else zero
                after = x[c + 1] if c < COLS - 1 else zero
                moved = jnp.where(lane >= LANES // 2, before, after)
                moved = pltpu.roll(moved, (base + part * 8 + WM) % LANES, 1)
                side = jnp.where(here, moved, side)
            sides[c] = side

    before = None
    for f in range(freqs):
        parts = products(f)
        if before is not None:
            place(f - 1, before)
        before = parts
    place(freqs - 1, before)
    me = lax.axis_index("refl")
    for p in range(rows):
        for c in range(COLS):
            g = p * COLS + c
            blocks[g, main : main + nb * 64, :] = bands[g].astype(BF16)
            side = [sides[c, p * WC : (p + 1) * WC, :]]
            for start in band_rows(p, rows):
                side.append(
                    jnp.zeros((WM, LANES), F32)
                    if start is None
                    else sides[c, start : start + WM, :]
                )
            side.append(jnp.zeros((16 - nb * WM, LANES), F32))
            blocks[g, main + nb * 64 :, :] = jnp.concatenate(side, 0).astype(BF16)
    for out, k in zip(outs, parcels(refl)):
        out[...] = blocks[((me ^ k) + 2) % refl]


def far_places(refl):
    return list(range(4, refl, 2))


def parcels(refl):
    far = far_places(refl)
    return [k ^ 1 for k in far] + far + [0, 1, 2, 3]


def block_terms(spectra, rows):
    refl = rows * COLS
    freqs, receivers, width = spectra.shape[1:]
    nb = len(band_rows(0, rows))
    size = 2 * HF * WC + nb * 64 + 48
    return pl.pallas_call(
        functools.partial(terms_kernel, rows),
        in_specs=[pl.BlockSpec(memory_space=pl.ANY)],
        out_shape=[jax.ShapeDtypeStruct((size, LANES), BF16)] * refl,
        scratch_shapes=[
            pltpu.VMEM((freqs, 2, receivers, width), BF16),
            pltpu.VMEM((refl, size, LANES), BF16),
            pltpu.VMEM((refl, nb * 64, LANES), F32),
            pltpu.VMEM((COLS, rows * WC, LANES), F32),
            pltpu.SemaphoreType.DMA((freqs, 2)),
        ],
        compiler_params=pltpu.CompilerParams(vmem_limit_bytes=TERMS_VMEM),
        name="block_terms",
    )(spectra)


def project_kernel(r_ref, t_ref, keep_ref, send_ref):
    j = lax.axis_index("freq")
    table = jnp.concatenate([t_ref[j, TIME], t_ref[1 - j, TIME]], 0).astype(BF16)
    half = WC // 2
    for s in range(half):
        pair = jnp.concatenate([r_ref[s], r_ref[half + s]], 0)
        got = lax.dot_general(table, pair, (((1,), (1,)), ((), ())), preferred_element_type=F32)
        keep_ref[s] = got[: 2 * HF]
        send_ref[s] = got[2 * HF :]


def project(recorded, table):
    shape = jax.ShapeDtypeStruct((WC // 2, 2 * HF, LANES), F32)
    return pl.pallas_call(
        project_kernel, out_shape=[shape, shape], compiler_params=VMEM, name="project"
    )(recorded, table)


def grid_place(rows):
    g = (lax.axis_index("refl") + 2) % (rows * COLS)
    return g // COLS, g % COLS


def edge_kernel(rows, keep_ref, other_ref, *outs):
    bands, sides_ref = outs[:-1], outs[-1]
    j = lax.axis_index("freq")
    p, _ = grid_place(rows)
    half = WC // 2
    low = lanes_of(HF) < LANES // 2

    def build(out_ref, first, upper):
        for s in range(WM):
            for part in range(2):
                rows_of = pl.ds(part * HF, HF)
                kept = keep_ref[first + s, rows_of, :]
                other = other_ref[first + s, rows_of, :]
                a = jnp.where(j == 0, kept, other)
                b = jnp.where(j == 0, other, kept)
                plain = jnp.where(low, a, pltpu.roll(b, LANES // 2, 1))
                shifted = jnp.where(low, pltpu.roll(a, LANES // 2, 1), b)
                band = jnp.where(upper, shifted, plain)
                out_ref[pl.ds(part * WM + s, HF, stride=8), :] = band

    if rows == 2:
        build(bands[0], jnp.where(p == 0, half - WM, 0), p == 0)
    else:
        build(bands[0], half - WM, True)
        build(bands[1], 0, False)

    keep = keep_ref[...].reshape(half * 2 * HF, LANES)
    other = other_ref[...].reshape(half * 2 * HF, LANES)
    left = jnp.where(j == 0, keep, other).astype(BF16)
    right = jnp.where(j == 0, other, keep).astype(BF16)
    row = lax.broadcasted_iota(jnp.int32, (LANES, LANES), 0)
    r = lax.broadcasted_iota(jnp.int32, (LANES, LANES), 1) % 8
    at = lax.broadcasted_iota(jnp.int32, (half, 2 * HF, LANES), 1)
    lane = lax.broadcasted_iota(jnp.int32, (half, 2 * HF, LANES), 2)
    mine = (lane // 16 == at % HF) & ((lane // 8) % 2 == at // HF)
    for upper in range(2):
        from_right = ((row == upper * 64 + 60 + r) & (r < WM)).astype(F32).astype(BF16)
        from_left = ((row == upper * 64 + r - WM) & (r >= WM)).astype(F32).astype(BF16)
        x = jnp.dot(left, from_left, preferred_element_type=F32)
        x = x + jnp.dot(right, from_right, preferred_element_type=F32)
        x = jnp.where(mine, x.reshape(half, 2 * HF, LANES), 0.0)
        sides_ref[upper * half : (upper + 1) * half, :] = jnp.sum(x, 1)


def edge_projections(keep, other, rows):
    nb = len(band_rows(0, rows))
    return pl.pallas_call(
        functools.partial(edge_kernel, rows),
        out_shape=[jax.ShapeDtypeStruct((64, LANES), F32)] * nb
        + [jax.ShapeDtypeStruct((WC, LANES), F32)],
        compiler_params=VMEM,
        name="edge_projections",
    )(keep, other)


def statistics_kernel(rows, *refs):
    nb = len(band_rows(0, rows))
    count = rows * COLS // 2 + 2
    blocks, refs = refs[:count], refs[count:]
    keep_ref, other_ref, lags_ref = refs[:3]
    rims = [x[...] for x in refs[3 : 3 + nb * 3 + 2]]
    bands, nears, fars = rims[:nb], rims[nb : 2 * nb + 1], rims[2 * nb + 1 :]
    refs = refs[3 + nb * 3 + 2 :]
    bands = [x.astype(F32) for x in bands]
    own_ref, send_ref, lag_ref, spectrum = refs
    j = lax.axis_index("freq")
    p, c = grid_place(rows)
    half = WC // 2

    def summed(start, size):
        total = blocks[0][start : start + size, :].astype(F32)
        for block in blocks[1:]:
            total = total + block[start : start + size, :].astype(F32)
        return total.astype(BF16).astype(F32)

    low = lanes_of(half) < LANES // 2
    for fp in range(2 * HF):
        x = summed(fp * WC, WC)
        a, b = x[:half], x[half:]
        first = jnp.where(low, a, pltpu.roll(b, LANES // 2, 1))
        second = jnp.where(low, pltpu.roll(a, LANES // 2, 1), b)
        spectrum[pl.ds(fp, half, stride=16), :] = first
        spectrum[pl.ds(half * 16 + fp, half, stride=16), :] = second
    count = half * 16
    here = pl.multiple_of(j * count, count)
    there = pl.multiple_of((1 - j) * count, count)
    own_ref[...] = spectrum[pl.ds(here, count), :].astype(BF16)
    send_ref[...] = spectrum[pl.ds(there, count), :].astype(BF16)
    sums = []
    for at, q_ref in ((here, keep_ref), (there, other_ref)):
        power = in_phase = turned = jnp.zeros((HF, LANES), F32)
        for s in range(half):
            a = spectrum[pl.ds(at + s * 16, HF), :]
            b = spectrum[pl.ds(at + s * 16 + HF, HF), :]
            qc, qs = q_ref[s, :HF, :], q_ref[s, HF:, :]
            power = power + (a * a + b * b)
            in_phase = in_phase + (a * qc + b * qs)
            turned = turned + (b * qc - a * qs)
        sums.append([power, in_phase, turned])
    total = None
    sub = lax.broadcasted_iota(jnp.int32, (HF, 8, LANES), 1)
    for n in range(nb):
        x = summed(2 * HF * WC + n * 64, 64).reshape(HF, 8, LANES)
        q = bands[n].reshape(HF, 8, LANES)
        partner = jnp.where(sub < WM, -1.0, 1.0) * pltpu.roll(q, WM, 1)
        here_sums = [jnp.sum(x * y, 1) for y in (x, q, partner)]
        total = here_sums if total is None else [a + b for a, b in zip(total, here_sums)]
    sums.append(total)

    window = lax.broadcasted_iota(jnp.int32, (8, LANES), 0)
    lane = lanes_of(8)
    window = jnp.where(window < 4, (window + 2 * j) % 4, 8)
    starts = window * WC - WM

    def mask(receiver):
        return ((receiver >= starts) & (receiver < starts + WC + 2 * WM)).astype(F32)

    dot = functools.partial(lax.dot_general, precision=EXACT, preferred_element_type=F32)
    stats = jnp.zeros((8, 32), F32)
    receivers = (j * 64 + lane % 64, (1 - j) * 64 + lane % 64, lane)
    for x, receiver in zip(sums, receivers):
        x = jnp.concatenate(x + [jnp.zeros((HF, LANES), F32)], 0)
        stats = stats + dot(mask(receiver), x, (((1,), (1,)), ((), ())))
    x = summed(2 * HF * WC + nb * 64, 48)
    l48 = lanes_of(48)
    from_near = ((l48 % 8) < WM) == ((c % 2) == 1)
    q = []
    for sides in (nears, fars):
        sides = [x.astype(F32) for x in sides]
        pieces = [sides[0]]
        for n, side in enumerate(sides[1:]):
            top, bottom = side[:WM, :], side[WC - WM :, :]
            pieces.append(jnp.where(p == 0, top, bottom) if nb == 1 else (bottom, top)[n])
        pieces.append(jnp.zeros((16 - nb * WM, LANES), F32))
        q.append(jnp.concatenate(pieces, 0))
    q = jnp.where(from_near, q[0], q[1])
    first_part = (l48 // 8) % 2 == 0
    partner = jnp.where(first_part, -pltpu.roll(q, LANES - 8, 1), pltpu.roll(q, 8, 1))
    row = lax.broadcasted_iota(jnp.int32, (LANES, 32), 0)
    column = lax.broadcasted_iota(jnp.int32, (LANES, 32), 1)
    at_side = ((window == 0) & (lane % 8 < WM)) | ((window == 3) & (lane % 8 >= WM))
    for n, y in enumerate((x, q, partner)):
        z = jnp.sum(x * y, 0, keepdims=True)
        z = jnp.where(at_side, jnp.broadcast_to(z, (8, LANES)), 0.0)
        to = (column == n * HF + row // 16).astype(F32)
        stats = stats + dot(z, to, (((1,), (0,)), ((), ())))
    lag_ref[...] = dot(stats, lags_ref[j, LAGS], (((1,), (0,)), ((), ())))


def statistics(blocks, keep, other, table, bands, nears, fars, rows):
    count = WC // 2 * 2 * HF
    return pl.pallas_call(
        functools.partial(statistics_kernel, rows),
        out_shape=[
            jax.ShapeDtypeStruct((count, LANES), BF16),
            jax.ShapeDtypeStruct((count, LANES), BF16),
            jax.ShapeDtypeStruct((8, 2 * LANES), F32),
        ],
        scratch_shapes=[pltpu.VMEM((2 * count, LANES), F32)],
        compiler_params=VMEM,
        name="statistics",
    )(*blocks, keep, other, table, *bands, *nears, *fars)


def subtract_kernel(
    steps,
    lag_ref,
    lag_got_ref,
    start_ref,
    table_ref,
    own_ref,
    got_ref,
    r_low_ref,
    r_high_ref,
    clean_ref,
    filters_ref,
    wavelets,
):
    step = pl.program_id(0)
    j = lax.axis_index("freq")
    half = WC // 2

    @pl.when(step == 0)
    def _():
        total = lag_ref[0:2, :] + lag_got_ref[2:4, :]
        lag, target = total[:, :LANES], total[:, LANES:]
        lane = lanes_of(2)
        held = lane < TAPS
        magnitude = jnp.where(held, jnp.abs(lag), 0.0)
        zero_lag = jnp.sum(jnp.where(lane == 0, lag, 0.0), 1, keepdims=True)
        others = jnp.sum(jnp.where(lane >= 1, magnitude, 0.0), 1, keepdims=True)
        step_size = 0.5 / (zero_lag + 2.0 * others + 1e-06)
        filters = jnp.concatenate(
            [start_ref[...], jnp.zeros((2, LANES - TAPS), F32)], 1
        )
        spread = [jnp.broadcast_to(lag[:, d : d + 1], (2, LANES)) for d in range(TAPS)]
        for repeat in range(ITERS):
            applied = spread[0] * filters
            for d in range(1, TAPS):
                applied = applied + spread[d] * (
                    pltpu.roll(filters, d, 1) + pltpu.roll(filters, LANES - d, 1)
                )
            filters = jnp.where(held, filters + step_size * (target - applied), 0.0)
        filters_ref[...] = filters[:, :TAPS]
        taps = filters.astype(BF16).astype(F32)
        for w in range(2):
            for n, h in enumerate((j, 1 - j)):
                tap = taps[w : w + 1, :]
                hc = jnp.sum(table_ref[h, TRIG, :LANES] * tap, 1, keepdims=True)
                hs = jnp.sum(table_ref[h, TRIG, LANES:] * tap, 1, keepdims=True)
                wave = hc * table_ref[h, TIME] + hs * table_ref[h, TURNED]
                at = w * 32 + n * 16
                wavelets[at : at + 16, :] = wave.astype(BF16)

    table = wavelets[...]
    lane = lax.broadcasted_iota(jnp.int32, (32, LANES), 1)
    first = (lane % 64) < WC
    zero = jnp.zeros((32, LANES), BF16)
    for s in range(half // steps):
        x = jnp.concatenate([own_ref[s * 16 : s * 16 + 16, :], got_ref[s * 16 : s * 16 + 16, :]], 0)
        both = jnp.concatenate([jnp.where(first, x, zero), jnp.where(first, zero, x)], 0)
        predicted = lax.dot_general(
            both, table, (((0,), (0,)), ((), ())), preferred_element_type=F32
        )
        clean_ref[0, s] = (r_low_ref[0, s].astype(F32) - predicted[:64]).astype(BF16)
        clean_ref[1, s] = (r_high_ref[0, s].astype(F32) - predicted[64:]).astype(BF16)


def subtract(lag, lag_got, start, table, own, got, recorded):
    steps = 1
    half = WC // 2
    each = half // steps
    recorded = recorded.reshape(2, half, 64, NT)
    whole = lambda x: pl.BlockSpec(x.shape, lambda i: (0,) * x.ndim)
    small = (lag, lag_got, start, table)
    rows_spec = pl.BlockSpec((each * 16, LANES), lambda i: (i, 0))
    return pl.pallas_call(
        functools.partial(subtract_kernel, steps),
        grid=(steps,),
        in_specs=[whole(x) for x in small]
        + [
            rows_spec,
            rows_spec,
            pl.BlockSpec((1, each, 64, NT), lambda i: (0, i, 0, 0)),
            pl.BlockSpec((1, each, 64, NT), lambda i: (1, i, 0, 0)),
        ],
        out_specs=[
            pl.BlockSpec((2, each, 64, NT), lambda i: (0, i, 0, 0)),
            pl.BlockSpec((2, TAPS), lambda i: (0, 0)),
        ],
        out_shape=[
            jax.ShapeDtypeStruct((2, half, 64, NT), BF16),
            jax.ShapeDtypeStruct((2, TAPS), F32),
        ],
        scratch_shapes=[pltpu.VMEM((64, NT), BF16)],
        compiler_params=VMEM,
        name="subtract",
    )(*small, own, got, recorded, recorded)


def body(spectra, recorded, initial_filters):
    refl = lax.axis_size("refl")
    rows = refl // COLS
    table = jnp.asarray(tables())
    core_swap = [(0, 1), (1, 0)]

    def place(p, c):
        return (p * COLS + c - 2) % refl

    def swap(x, k):
        return lax.ppermute(x, "refl", [(i, i ^ k) for i in range(refl)])

    def add(x, y):
        return (x.astype(F32) + y.astype(F32)).astype(BF16)

    after = lax.optimization_barrier
    blocks = block_terms(spectra, rows)
    far = far_places(refl)
    sent, kept, close = list(blocks[: len(far)]), blocks[len(far) : -4], blocks[-4:]
    came = [swap(sent[0], 1)]
    tile, sent[1] = after((recorded[0, 0], sent[1]))
    keep, send = project(tile, table)
    other = lax.ppermute(send, "freq", core_swap)
    *bands, sides = edge_projections(keep, other, rows)
    extra = {}
    if rows == 2:
        near = swap(sides, 1)
        extra = {6: [near], 4: [bands[0], near], 3: [sides]}

    def parcel(block, k):
        return jnp.concatenate([block] + [x.astype(BF16) for x in extra.get(k, [])])

    totals = [parcel(add(kept[0], came[0]), far[0])]
    totals[0], *sent[1:] = after((totals[0], *sent[1:]))
    came += [swap(x, 1) for x in sent[1:]]
    totals += [parcel(add(kept[n], came[n]), far[n]) for n in range(1, len(far))]
    got = [swap(x, k) for x, k in zip(totals, far)]
    own, *close = close
    close, _ = after((close, totals[0]))
    close = [swap(parcel(x, k), k) for k, x in enumerate(close, 1)]
    size = own.shape[0]
    if rows == 2:
        bands = [got[0][size : size + 64]]
        nears, fars = [near, got[0][size + 64 :]], [got[1][size:], close[2][size:]]
    else:

        def shift(x, rise, across):
            route = [
                (place(p, c), place(p + rise, across[c]))
                for p in range(rows)
                for c in range(COLS)
                if 0 <= p + rise < rows and across[c] is not None
            ]
            return lax.ppermute(x, "refl", route)

        bands = [shift(x, rise, (0, 1, 2, 3)) for x, rise in zip(bands, (1, -1))]
        nears = [shift(sides, rise, (1, 0, 3, 2)) for rise in (0, 1, -1)]
        fars = [shift(sides, rise, (None, 2, 1, None)) for rise in (0, 1, -1)]
    own, away, lag = statistics([own] + got + close, keep, other, table, bands, nears, fars, rows)
    away_got = lax.ppermute(away, "freq", core_swap)
    lag_got = lax.ppermute(lag, "freq", core_swap)
    clean, filters = subtract(
        lag,
        lag_got,
        initial_filters.reshape(2, TAPS),
        table,
        own,
        away_got,
        tile,
    )
    return (clean.reshape(recorded.shape), filters.reshape(initial_filters.shape))


def solution(mesh):
    placed = (
        P(None, "freq", "groups", "refl"),
        P("refl", "freq", "groups", None, None),
        P("refl", "freq", "groups", None, None),
    )
    return jax.shard_map(
        body,
        mesh=mesh,
        in_specs=placed,
        out_specs=(
            P("refl", "freq", "groups", None, None),
            P("refl", "freq", "groups", None, None),
        ),
        check_vma=False,
    )
```

```python
import functools
import math

import jax
import jax.numpy as jnp
import numpy as np
from jax import lax
from jax.experimental import pallas as pl
from jax.experimental.pallas import tpu as pltpu
from jax.sharding import PartitionSpec as P

NF = 16
K0 = 48
NT = 256
XR = 8192
WC = 32
WM = 4
TAPS = 33
ITERS = 3
HALF = (TAPS - 1) // 2
COLS = 4
LANES = 128
HF = 8
TERMS_VMEM = 48 * 1024 * 1024
AHEAD = 3
EXACT = lax.Precision.HIGHEST
F32 = jnp.float32
BF16 = jnp.bfloat16
VMEM = pltpu.CompilerParams(vmem_limit_bytes=12 * 1024 * 1024)


def tables():
    f = np.arange(NF)
    t = np.arange(NT)
    w = 2.0 * np.pi * (K0 + f) / NT
    angle = 2.0 * np.pi * (((K0 + f)[:, None] * t[None, :]) % NT) / NT
    weight = math.sqrt(2.0 / NF)
    table = np.stack([weight * np.cos(angle), -weight * np.sin(angle)], 1)
    table = table.astype(np.float32).astype(jnp.bfloat16).astype(np.float32)
    halves = table.reshape(2, HF, 2, NT).transpose(0, 2, 1, 3)
    time = halves.reshape(2, 2 * HF, NT)
    turned = np.stack([-halves[:, 1], halves[:, 0]], 1).reshape(2, 2 * HF, NT)
    lane = np.arange(LANES)
    held = lane < TAPS
    tap = lane - HALF
    cos_k = np.where(held, np.cos(w[:, None] * tap), 0.0).reshape(2, HF, LANES)
    sin_k = np.where(held, np.sin(w[:, None] * tap), 0.0).reshape(2, HF, LANES)
    lag = np.where(held, 16.0 * np.cos(w[:, None] * lane), 0.0).reshape(2, HF, LANES)
    zero = np.zeros_like(lag)
    to_lag = np.concatenate([lag, zero, zero, zero], 1)
    to_target = np.concatenate([zero, cos_k, sin_k, zero], 1)
    lags = np.concatenate([to_lag, to_target], 2)
    trig = np.concatenate([np.concatenate([cos_k, cos_k], 1), np.concatenate([sin_k, sin_k], 1)], 2)
    return np.concatenate([time, turned, lags, trig], 1).astype(np.float32)


TIME, TURNED, LAGS, TRIG = (slice(0, 16), slice(16, 32), slice(32, 64), slice(64, 80))


def lanes_of(rows):
    return lax.broadcasted_iota(jnp.int32, (rows, LANES), 1)


def band_rows(p, rows):
    if rows == 2:
        return [WC if p == 0 else WC - WM]
    return [p * WC - WM if p > 0 else None, (p + 1) * WC if p < rows - 1 else None]


def terms_kernel(rows, s_hbm, *rest):
    refl = rows * COLS
    outs, (buffer, blocks, bands, sides, arrived) = rest[:-5], rest[-5:]
    sources = rows * WC
    freqs, _, _, width = buffer.shape
    amplitude = 1.0 / math.sqrt(2.0 * XR)
    nb = len(band_rows(0, rows))
    main = 2 * HF * WC

    def fetch(f, part):
        return pltpu.make_async_copy(s_hbm.at[part, f], buffer.at[f, part], arrived.at[f, part])

    for f in range(AHEAD):
        for part in range(2):
            fetch(f, part).start()

    def products(f):
        if f + AHEAD < freqs:
            for part in range(2):
                fetch(f + AHEAD, part).start()
        for part in range(2):
            fetch(f, part).wait()
        left = buffer[f, :, :sources, :].reshape(2 * sources, width)
        parts = [[], []]
        for c in range(COLS):
            right = buffer[f, :, c * LANES : (c + 1) * LANES, :].reshape(2 * LANES, width)
            got = lax.dot_general(left, right, (((1,), (1,)), ((), ())), preferred_element_type=F32)
            parts[0].append(amplitude * (got[:sources, :LANES] - got[sources:, LANES:]))
            parts[1].append(amplitude * (got[:sources, LANES:] + got[sources:, :LANES]))
        return parts

    def place(f, parts):
        for c in range(COLS):
            for p in range(rows):
                g = p * COLS + c
                for part in range(2):
                    at = part * HF * WC + f * WC
                    x = parts[part][c][p * WC : (p + 1) * WC]
                    blocks[g, at : at + WC, :] = x.astype(BF16)
                for n, start in enumerate(band_rows(p, rows)):
                    if start is None:
                        band = jnp.zeros((2 * WM, LANES), F32)
                    else:
                        band = jnp.concatenate([x[c][start : start + WM] for x in parts], 0)
                    bands[g, n * HF * 8 + f * 8 : n * HF * 8 + f * 8 + 8, :] = band
        lane = lanes_of(sources)
        base = f * 16
        first = (lane >= base) & (lane < base + 8)
        second = (lane >= base + 8) & (lane < base + 16)
        zero = jnp.zeros((sources, LANES), F32)
        for c in range(COLS):
            side = sides[c]
            for part, here in enumerate((first, second)):
                x = parts[part]
                before = x[c - 1] if c > 0 else zero
                after = x[c + 1] if c < COLS - 1 else zero
                moved = jnp.where(lane >= LANES // 2, before, after)
                moved = pltpu.roll(moved, (base + part * 8 + WM) % LANES, 1)
                side = jnp.where(here, moved, side)
            sides[c] = side

    before = None
    for f in range(freqs):
        parts = products(f)
        if before is not None:
            place(f - 1, before)
        before = parts
    place(freqs - 1, before)
    me = lax.axis_index("refl")
    for p in range(rows):
        for c in range(COLS):
            g = p * COLS + c
            blocks[g, main : main + nb * 64, :] = bands[g].astype(BF16)
            side = [sides[c, p * WC : (p + 1) * WC, :]]
            for start in band_rows(p, rows):
                side.append(
                    jnp.zeros((WM, LANES), F32)
                    if start is None
                    else sides[c, start : start + WM, :]
                )
            side.append(jnp.zeros((16 - nb * WM, LANES), F32))
            blocks[g, main + nb * 64 :, :] = jnp.concatenate(side, 0).astype(BF16)
    for out, k in zip(outs, parcels(refl)):
        out[...] = blocks[((me ^ k) + 2) % refl]


def far_places(refl):
    return list(range(4, refl, 2))


def parcels(refl):
    far = far_places(refl)
    return [k ^ 1 for k in far] + far + [0, 1, 2, 3]


def block_terms(spectra, rows):
    refl = rows * COLS
    freqs, receivers, width = spectra.shape[1:]
    nb = len(band_rows(0, rows))
    size = 2 * HF * WC + nb * 64 + 48
    return pl.pallas_call(
        functools.partial(terms_kernel, rows),
        in_specs=[pl.BlockSpec(memory_space=pl.ANY)],
        out_shape=[jax.ShapeDtypeStruct((size, LANES), BF16)] * refl,
        scratch_shapes=[
            pltpu.VMEM((freqs, 2, receivers, width), BF16),
            pltpu.VMEM((refl, size, LANES), BF16),
            pltpu.VMEM((refl, nb * 64, LANES), F32),
            pltpu.VMEM((COLS, rows * WC, LANES), F32),
            pltpu.SemaphoreType.DMA((freqs, 2)),
        ],
        compiler_params=pltpu.CompilerParams(vmem_limit_bytes=TERMS_VMEM),
        name="block_terms",
    )(spectra)


def project_kernel(r_ref, t_ref, keep_ref, send_ref):
    j = lax.axis_index("freq")
    table = jnp.concatenate([t_ref[j, TIME], t_ref[1 - j, TIME]], 0).astype(BF16)
    half = WC // 2
    for s in range(half):
        pair = jnp.concatenate([r_ref[s], r_ref[half + s]], 0)
        got = lax.dot_general(table, pair, (((1,), (1,)), ((), ())), preferred_element_type=F32)
        keep_ref[s] = got[: 2 * HF]
        send_ref[s] = got[2 * HF :]


def project(recorded, table):
    shape = jax.ShapeDtypeStruct((WC // 2, 2 * HF, LANES), F32)
    return pl.pallas_call(
        project_kernel, out_shape=[shape, shape], compiler_params=VMEM, name="project"
    )(recorded, table)


def grid_place(rows):
    g = (lax.axis_index("refl") + 2) % (rows * COLS)
    return g // COLS, g % COLS


def edge_kernel(rows, keep_ref, other_ref, *outs):
    bands, sides_ref = outs[:-1], outs[-1]
    j = lax.axis_index("freq")
    p, _ = grid_place(rows)
    half = WC // 2
    low = lanes_of(HF) < LANES // 2

    def build(out_ref, first, upper):
        for s in range(WM):
            for part in range(2):
                rows_of = pl.ds(part * HF, HF)
                kept = keep_ref[first + s, rows_of, :]
                other = other_ref[first + s, rows_of, :]
                a = jnp.where(j == 0, kept, other)
                b = jnp.where(j == 0, other, kept)
                plain = jnp.where(low, a, pltpu.roll(b, LANES // 2, 1))
                shifted = jnp.where(low, pltpu.roll(a, LANES // 2, 1), b)
                band = jnp.where(upper, shifted, plain)
                out_ref[pl.ds(part * WM + s, HF, stride=8), :] = band

    if rows == 2:
        build(bands[0], jnp.where(p == 0, half - WM, 0), p == 0)
    else:
        build(bands[0], half - WM, True)
        build(bands[1], 0, False)

    keep = keep_ref[...].reshape(half * 2 * HF, LANES)
    other = other_ref[...].reshape(half * 2 * HF, LANES)
    left = jnp.where(j == 0, keep, other).astype(BF16)
    right = jnp.where(j == 0, other, keep).astype(BF16)
    row = lax.broadcasted_iota(jnp.int32, (LANES, LANES), 0)
    r = lax.broadcasted_iota(jnp.int32, (LANES, LANES), 1) % 8
    at = lax.broadcasted_iota(jnp.int32, (half, 2 * HF, LANES), 1)
    lane = lax.broadcasted_iota(jnp.int32, (half, 2 * HF, LANES), 2)
    mine = (lane // 16 == at % HF) & ((lane // 8) % 2 == at // HF)
    for upper in range(2):
        from_right = ((row == upper * 64 + 60 + r) & (r < WM)).astype(F32).astype(BF16)
        from_left = ((row == upper * 64 + r - WM) & (r >= WM)).astype(F32).astype(BF16)
        x = jnp.dot(left, from_left, preferred_element_type=F32)
        x = x + jnp.dot(right, from_right, preferred_element_type=F32)
        x = jnp.where(mine, x.reshape(half, 2 * HF, LANES), 0.0)
        sides_ref[upper * half : (upper + 1) * half, :] = jnp.sum(x, 1)


def edge_projections(keep, other, rows):
    nb = len(band_rows(0, rows))
    return pl.pallas_call(
        functools.partial(edge_kernel, rows),
        out_shape=[jax.ShapeDtypeStruct((64, LANES), F32)] * nb
        + [jax.ShapeDtypeStruct((WC, LANES), F32)],
        compiler_params=VMEM,
        name="edge_projections",
    )(keep, other)


def statistics_kernel(rows, *refs):
    nb = len(band_rows(0, rows))
    count = rows * COLS // 2 + 2
    blocks, refs = refs[:count], refs[count:]
    keep_ref, other_ref, lags_ref = refs[:3]
    rims = [x[...] for x in refs[3 : 3 + nb * 3 + 2]]
    bands, nears, fars = rims[:nb], rims[nb : 2 * nb + 1], rims[2 * nb + 1 :]
    refs = refs[3 + nb * 3 + 2 :]
    bands = [x.astype(F32) for x in bands]
    own_ref, send_ref, lag_ref, spectrum = refs
    j = lax.axis_index("freq")
    p, c = grid_place(rows)
    half = WC // 2

    def summed(start, size):
        total = blocks[0][start : start + size, :].astype(F32)
        for block in blocks[1:]:
            total = total + block[start : start + size, :].astype(F32)
        return total.astype(BF16).astype(F32)

    low = lanes_of(half) < LANES // 2
    for fp in range(2 * HF):
        x = summed(fp * WC, WC)
        a, b = x[:half], x[half:]
        first = jnp.where(low, a, pltpu.roll(b, LANES // 2, 1))
        second = jnp.where(low, pltpu.roll(a, LANES // 2, 1), b)
        spectrum[pl.ds(fp, half, stride=16), :] = first
        spectrum[pl.ds(half * 16 + fp, half, stride=16), :] = second
    count = half * 16
    here = pl.multiple_of(j * count, count)
    there = pl.multiple_of((1 - j) * count, count)
    own_ref[...] = spectrum[pl.ds(here, count), :].astype(BF16)
    send_ref[:count, :] = spectrum[pl.ds(there, count), :]
    sums = []
    for at, q_ref in ((here, keep_ref), (there, other_ref)):
        power = in_phase = turned = jnp.zeros((HF, LANES), F32)
        for s in range(half):
            a = spectrum[pl.ds(at + s * 16, HF), :]
            b = spectrum[pl.ds(at + s * 16 + HF, HF), :]
            qc, qs = q_ref[s, :HF, :], q_ref[s, HF:, :]
            power = power + (a * a + b * b)
            in_phase = in_phase + (a * qc + b * qs)
            turned = turned + (b * qc - a * qs)
        sums.append([power, in_phase, turned])
    total = None
    sub = lax.broadcasted_iota(jnp.int32, (HF, 8, LANES), 1)
    for n in range(nb):
        x = summed(2 * HF * WC + n * 64, 64).reshape(HF, 8, LANES)
        q = bands[n].reshape(HF, 8, LANES)
        partner = jnp.where(sub < WM, -1.0, 1.0) * pltpu.roll(q, WM, 1)
        here_sums = [jnp.sum(x * y, 1) for y in (x, q, partner)]
        total = here_sums if total is None else [a + b for a, b in zip(total, here_sums)]
    sums.append(total)

    window = lax.broadcasted_iota(jnp.int32, (8, LANES), 0)
    lane = lanes_of(8)
    window = jnp.where(window < 4, (window + 2 * j) % 4, 8)
    starts = window * WC - WM

    def mask(receiver):
        return ((receiver >= starts) & (receiver < starts + WC + 2 * WM)).astype(F32)

    dot = functools.partial(lax.dot_general, precision=EXACT, preferred_element_type=F32)
    stats = jnp.zeros((8, 32), F32)
    receivers = (j * 64 + lane % 64, (1 - j) * 64 + lane % 64, lane)
    for x, receiver in zip(sums, receivers):
        x = jnp.concatenate(x + [jnp.zeros((HF, LANES), F32)], 0)
        stats = stats + dot(mask(receiver), x, (((1,), (1,)), ((), ())))
    x = summed(2 * HF * WC + nb * 64, 48)
    l48 = lanes_of(48)
    from_near = ((l48 % 8) < WM) == ((c % 2) == 1)
    q = []
    for sides in (nears, fars):
        sides = [x.astype(F32) for x in sides]
        pieces = [sides[0]]
        for n, side in enumerate(sides[1:]):
            top, bottom = side[:WM, :], side[WC - WM :, :]
            pieces.append(jnp.where(p == 0, top, bottom) if nb == 1 else (bottom, top)[n])
        pieces.append(jnp.zeros((16 - nb * WM, LANES), F32))
        q.append(jnp.concatenate(pieces, 0))
    q = jnp.where(from_near, q[0], q[1])
    first_part = (l48 // 8) % 2 == 0
    partner = jnp.where(first_part, -pltpu.roll(q, LANES - 8, 1), pltpu.roll(q, 8, 1))
    row = lax.broadcasted_iota(jnp.int32, (LANES, 32), 0)
    column = lax.broadcasted_iota(jnp.int32, (LANES, 32), 1)
    at_side = ((window == 0) & (lane % 8 < WM)) | ((window == 3) & (lane % 8 >= WM))
    for n, y in enumerate((x, q, partner)):
        z = jnp.sum(x * y, 0, keepdims=True)
        z = jnp.where(at_side, jnp.broadcast_to(z, (8, LANES)), 0.0)
        to = (column == n * HF + row // 16).astype(F32)
        stats = stats + dot(z, to, (((1,), (0,)), ((), ())))
    lag = dot(stats, lags_ref[j, LAGS], (((1,), (0,)), ((), ())))
    lag_ref[...] = lag
    send_ref[count : count + 8, :] = lag[:, :LANES]
    send_ref[count + 8 :, :] = lag[:, LANES:]


def statistics(blocks, keep, other, table, bands, nears, fars, rows):
    count = WC // 2 * 2 * HF
    return pl.pallas_call(
        functools.partial(statistics_kernel, rows),
        out_shape=[
            jax.ShapeDtypeStruct((count, LANES), BF16),
            jax.ShapeDtypeStruct((count + 16, LANES), F32),
            jax.ShapeDtypeStruct((8, 2 * LANES), F32),
        ],
        scratch_shapes=[pltpu.VMEM((2 * count, LANES), F32)],
        compiler_params=VMEM,
        name="statistics",
    )(*blocks, keep, other, table, *bands, *nears, *fars)


def subtract_kernel(
    steps,
    lag_ref,
    start_ref,
    table_ref,
    own_ref,
    got_ref,
    r_low_ref,
    r_high_ref,
    clean_ref,
    filters_ref,
    wavelets,
):
    step = pl.program_id(0)
    j = lax.axis_index("freq")
    half = WC // 2

    @pl.when(step == 0)
    def _():
        at = half * 16
        lag = lag_ref[0:2, :LANES] + got_ref[at + 2 : at + 4, :]
        target = lag_ref[0:2, LANES:] + got_ref[at + 10 : at + 12, :]
        lane = lanes_of(2)
        held = lane < TAPS
        magnitude = jnp.where(held, jnp.abs(lag), 0.0)
        zero_lag = jnp.sum(jnp.where(lane == 0, lag, 0.0), 1, keepdims=True)
        others = jnp.sum(jnp.where(lane >= 1, magnitude, 0.0), 1, keepdims=True)
        step_size = 0.5 / (zero_lag + 2.0 * others + 1e-06)
        filters = jnp.concatenate(
            [start_ref[...], jnp.zeros((2, LANES - TAPS), F32)], 1
        )
        spread = [jnp.broadcast_to(lag[:, d : d + 1], (2, LANES)) for d in range(TAPS)]
        for repeat in range(ITERS):
            applied = spread[0] * filters
            for d in range(1, TAPS):
                applied = applied + spread[d] * (
                    pltpu.roll(filters, d, 1) + pltpu.roll(filters, LANES - d, 1)
                )
            filters = jnp.where(held, filters + step_size * (target - applied), 0.0)
        filters_ref[...] = filters[:, :TAPS]
        taps = filters.astype(BF16).astype(F32)
        for w in range(2):
            for n, h in enumerate((j, 1 - j)):
                tap = taps[w : w + 1, :]
                hc = jnp.sum(table_ref[h, TRIG, :LANES] * tap, 1, keepdims=True)
                hs = jnp.sum(table_ref[h, TRIG, LANES:] * tap, 1, keepdims=True)
                wave = hc * table_ref[h, TIME] + hs * table_ref[h, TURNED]
                at = w * 32 + n * 16
                wavelets[at : at + 16, :] = wave.astype(BF16)

    table = wavelets[...]
    lane = lax.broadcasted_iota(jnp.int32, (32, LANES), 1)
    first = (lane % 64) < WC
    zero = jnp.zeros((32, LANES), BF16)
    for s in range(half // steps):
        x = jnp.concatenate([own_ref[s * 16 : s * 16 + 16, :], got_ref[s * 16 : s * 16 + 16, :].astype(BF16)], 0)
        both = jnp.concatenate([jnp.where(first, x, zero), jnp.where(first, zero, x)], 0)
        predicted = lax.dot_general(
            both, table, (((0,), (0,)), ((), ())), preferred_element_type=F32
        )
        clean_ref[0, s] = (r_low_ref[0, s].astype(F32) - predicted[:64]).astype(BF16)
        clean_ref[1, s] = (r_high_ref[0, s].astype(F32) - predicted[64:]).astype(BF16)


def subtract(lag, start, table, own, got, recorded):
    steps = 1
    half = WC // 2
    each = half // steps
    recorded = recorded.reshape(2, half, 64, NT)
    whole = lambda x: pl.BlockSpec(x.shape, lambda i: (0,) * x.ndim)
    small = (lag, start, table)
    rows_spec = pl.BlockSpec((each * 16, LANES), lambda i: (i, 0))
    return pl.pallas_call(
        functools.partial(subtract_kernel, steps),
        grid=(steps,),
        in_specs=[whole(x) for x in small]
        + [
            rows_spec,
            whole(got),
            pl.BlockSpec((1, each, 64, NT), lambda i: (0, i, 0, 0)),
            pl.BlockSpec((1, each, 64, NT), lambda i: (1, i, 0, 0)),
        ],
        out_specs=[
            pl.BlockSpec((2, each, 64, NT), lambda i: (0, i, 0, 0)),
            pl.BlockSpec((2, TAPS), lambda i: (0, 0)),
        ],
        out_shape=[
            jax.ShapeDtypeStruct((2, half, 64, NT), BF16),
            jax.ShapeDtypeStruct((2, TAPS), F32),
        ],
        scratch_shapes=[pltpu.VMEM((64, NT), BF16)],
        compiler_params=VMEM,
        name="subtract",
    )(*small, own, got, recorded, recorded)


def body(spectra, recorded, initial_filters):
    refl = lax.axis_size("refl")
    rows = refl // COLS
    table = jnp.asarray(tables())
    core_swap = [(0, 1), (1, 0)]

    def place(p, c):
        return (p * COLS + c - 2) % refl

    def swap(x, k):
        return lax.ppermute(x, "refl", [(i, i ^ k) for i in range(refl)])

    def add(x, y):
        return (x.astype(F32) + y.astype(F32)).astype(BF16)

    after = lax.optimization_barrier
    blocks = block_terms(spectra, rows)
    far = far_places(refl)
    sent, kept, close = list(blocks[: len(far)]), blocks[len(far) : -4], blocks[-4:]
    came = [swap(sent[0], 1)]
    tile, sent[1] = after((recorded[0, 0], sent[1]))
    keep, send = project(tile, table)
    other = lax.ppermute(send, "freq", core_swap)
    *bands, sides = edge_projections(keep, other, rows)
    extra = {}
    if rows == 2:
        near = swap(sides, 1)
        extra = {6: [near], 4: [bands[0], near], 3: [sides]}

    def parcel(block, k):
        return jnp.concatenate([block] + [x.astype(BF16) for x in extra.get(k, [])])

    totals = [parcel(add(kept[0], came[0]), far[0])]
    totals[0], *sent[1:] = after((totals[0], *sent[1:]))
    came += [swap(x, 1) for x in sent[1:]]
    totals += [parcel(add(kept[n], came[n]), far[n]) for n in range(1, len(far))]
    got = [swap(x, k) for x, k in zip(totals, far)]
    own, *close = close
    close, _ = after((close, totals[0]))
    close = [swap(parcel(x, k), k) for k, x in enumerate(close, 1)]
    size = own.shape[0]
    if rows == 2:
        bands = [got[0][size : size + 64]]
        nears, fars = [near, got[0][size + 64 :]], [got[1][size:], close[2][size:]]
    else:

        def shift(x, rise, across):
            route = [
                (place(p, c), place(p + rise, across[c]))
                for p in range(rows)
                for c in range(COLS)
                if 0 <= p + rise < rows and across[c] is not None
            ]
            return lax.ppermute(x, "refl", route)

        bands = [shift(x, rise, (0, 1, 2, 3)) for x, rise in zip(bands, (1, -1))]
        nears = [shift(sides, rise, (1, 0, 3, 2)) for rise in (0, 1, -1)]
        fars = [shift(sides, rise, (None, 2, 1, None)) for rise in (0, 1, -1)]
    own, away, lag = statistics([own] + got + close, keep, other, table, bands, nears, fars, rows)
    away_got = lax.ppermute(away, "freq", core_swap)
    clean, filters = subtract(
        lag,
        initial_filters.reshape(2, TAPS),
        table,
        own,
        away_got,
        tile,
    )
    return (clean.reshape(recorded.shape), filters.reshape(initial_filters.shape))


def solution(mesh):
    placed = (
        P(None, "freq", "groups", "refl"),
        P("refl", "freq", "groups", None, None),
        P("refl", "freq", "groups", None, None),
    )
    return jax.shard_map(
        body,
        mesh=mesh,
        in_specs=placed,
        out_specs=(
            P("refl", "freq", "groups", None, None),
            P("refl", "freq", "groups", None, None),
        ),
        check_vma=False,
    )
```
